128 devices in a mesh: gx: 16 (over x, z_hi, core), gy: 8 (over z_lo, y).
Axes of the slice: x: 4, y: 4, z: 4 (z_hi: 2, z_lo: 2; z = z_hi * 2 + z_lo), core: 2. Of those that a mesh axis runs over, the one named last changes fastest.
Arguments:
- source_mass: float32 [32, 8, 8, 1024], P('gx', None, None, 'gy'), may hold values from 0.1 to 2
- alpha_start: float32 [32, 8, 8, 1024], P('gx', None, None, 'gy'), may hold values from -4 to 220
- part_start: float32 [32, 24, 24, 1024], P('gx', None, None, 'gy'), may hold values from 0.01 to 0.3
Outputs:
- alpha_final: float32 [32, 8, 8, 1024], P('gx', None, None, 'gy')
- partials_final: float32 [32, 24, 24, 1024], P('gx', None, None, 'gy')
The draws below stay inside these ranges and needn't reach their ends.
All inputs are finite; a program needn't handle non-finite values.
Results may differ from the reference program's by a relative error of at most 0.00022.
Values sent between devices are 32-bit elements; how exact they have to be, the bound alone decides.
A program may use at most 64 MiB of HBM per device.

```python
import math
import jax
import jax.numpy as jnp
from jax import lax

CELL = 8
WIN = 24
ITERS = 2
PAIRS = 1
NCC = 32
NCR = 1024


def draw_alpha_start(key, part):
    key = jax.random.fold_in(key, 7)
    subkeys = jax.random.split(key, 1)
    full_shape = (NCC, CELL, CELL, NCR)
    return jax.random.truncated_normal(subkeys[0], -4.0, 4.0, full_shape, jnp.float32)


def block_scale(own_key, extent, cuts, low, top_value):
    level, own = 1.0, jax.random.fold_in(own_key, 6)
    for axis_at, parts in cuts:
        draws = jnp.exp(jax.random.uniform(jax.random.fold_in(own, axis_at), (parts,), jnp.float32, low / len(cuts), top_value / len(cuts)))
        level = level * jnp.repeat(draws, extent[axis_at] // parts).reshape([-1 if axis == axis_at else 1 for axis in range(len(extent))])
    return level


def setup_inputs(seed: int = 0) -> dict:
    arg_keys = jax.random.split(jax.random.key(seed), 4)
    return {
        "source_mass": jnp.clip(jnp.exp(math.log(2.0) - 2.9957323 * jax.random.uniform(arg_keys[0], (NCC, CELL, CELL, NCR), jnp.float32) ** block_scale(arg_keys[0], (NCC, CELL, CELL, NCR), ((0, 16), (3, 8)), -0.2, 0.2)), 0.1, 2.0),
        "alpha_start": draw_alpha_start(jax.random.fold_in(arg_keys[3], 71), 0),
        "part_start": jnp.clip(jnp.exp(math.log(0.3) - 3.4011974 * jax.random.uniform(arg_keys[2], (NCC, WIN, WIN, NCR), jnp.float32) ** block_scale(arg_keys[2], (NCC, WIN, WIN, NCR), ((0, 16), (3, 8)), -0.2, 0.2)), 0.01, 0.3),
    }


inverse_blur = 1.0 / 32.0


def log_sum_axis(values, axis):
    largest = jnp.max(values, axis=axis, keepdims=True)
    steady = jnp.where(jnp.isfinite(largest), largest, 0.0)
    summed = jnp.sum(jnp.exp(values - steady), axis=axis)
    return jnp.squeeze(steady, axis=axis) + jnp.log(summed)


def cost_table(cell_size):
    source_pos = jnp.arange(cell_size, dtype=jnp.float32)[:, None] + cell_size
    target_pos = jnp.arange(3 * cell_size, dtype=jnp.float32)[None, :]
    return inverse_blur * (source_pos - target_pos) ** 2


def cell_sums(potential, cost_rows):
    inner_sum = log_sum_axis(potential[:, :, :, None, :] - cost_rows[None, None, :, :, None], 2)
    return log_sum_axis(inner_sum[:, :, None, :, :] - cost_rows[None, :, :, None, None], 1)


def combine(values, cell_size, fill_value):
    window_size = values.shape[1]
    paired = values.reshape(2, window_size, window_size, values.shape[3] // 2, 2)
    placed = []
    for shift_u in range(2):
        for shift_v in range(2):
            pad_spec = ((cell_size * shift_u, cell_size * (1 - shift_u)), (cell_size * shift_v, cell_size * (1 - shift_v)), (0, 0))
            placed.append(jnp.pad(paired[shift_u, :, :, :, shift_v], pad_spec, constant_values=fill_value))
    return placed


def windows(target_pot, cell_size, window_size):
    row_blocks = []
    for shift_u in range(2):
        side_blocks = [target_pot[cell_size * shift_u:cell_size * shift_u + window_size, cell_size * shift_v:cell_size * shift_v + window_size] for shift_v in range(2)]
        row_blocks.append(jnp.stack(side_blocks, axis=-1).reshape(window_size, window_size, -1))
    return jnp.stack(row_blocks, axis=0)


def source_update(log_mass, window_pot, cost_rows):
    inner_sum = log_sum_axis(window_pot[:, :, None, :, :] - cost_rows[None, None, :, :, None], 3)
    outer_sum = log_sum_axis(inner_sum[:, None, :, :, :] - cost_rows[None, :, :, None, None], 2)
    return log_mass - outer_sum


def solve_block(block_mass, block_pot, block_part, cost_rows, iterations):
    cell_size = cost_rows.shape[0]
    window_size = cost_rows.shape[1]
    log_mass = jnp.log(block_mass)
    placed = combine(block_part, cell_size, 0.0)
    log_target = jnp.log(placed[0] + placed[1] + placed[2] + placed[3])
    potential = block_pot
    for repeat in range(iterations):
        target_pot = log_target - log_sum_axis(jnp.stack(combine(cell_sums(potential, cost_rows), cell_size, -jnp.inf), axis=0), 0)
        potential = source_update(log_mass, windows(target_pot, cell_size, window_size), cost_rows)
    sums_now = cell_sums(potential, cost_rows)
    target_pot = log_target - log_sum_axis(jnp.stack(combine(sums_now, cell_size, -jnp.inf), axis=0), 0)
    return potential, jnp.exp(windows(target_pot, cell_size, window_size) + sums_now)


def sweep(source_mass, potential, partials, iterations):
    cell_size = source_mass.shape[1]
    window_size = partials.shape[1]
    cost_rows = cost_table(cell_size)
    halves = source_mass.shape[0] // 2
    columns = source_mass.shape[3]

    def one_block(blocks):
        return solve_block(blocks[0], blocks[1], blocks[2], cost_rows, iterations)

    new_pot, new_part = lax.map(one_block, (source_mass.reshape(halves, 2, cell_size, cell_size, columns), potential.reshape(halves, 2, cell_size, cell_size, columns), partials.reshape(halves, 2, window_size, window_size, columns)))
    return new_pot.reshape(source_mass.shape), new_part.reshape(partials.shape)


def reference(source_mass, alpha_start, part_start):
    potential, partials = alpha_start, part_start
    for repeat in range(PAIRS):
        potential, partials = sweep(source_mass, potential, partials, ITERS)
        rolled = [jnp.roll(jnp.roll(tensor, -1, axis=0), -1, axis=3) for tensor in (source_mass, potential, partials)]
        new_pot, new_part = sweep(rolled[0], rolled[1], rolled[2], ITERS)
        potential = jnp.roll(jnp.roll(new_pot, 1, axis=0), 1, axis=3)
        partials = jnp.roll(jnp.roll(new_part, 1, axis=0), 1, axis=3)
    return potential, partials
```

```python
import functools
import math

import jax
import jax.numpy as jnp
import ml_dtypes
import numpy as np
from jax import lax
from jax.experimental import pallas as pl
from jax.experimental.pallas import tpu as pltpu
from jax.sharding import PartitionSpec as P

ITERS = 2
LANES = 128
MESH = pl.DeviceIdType.MESH
LN2_HI = 0.693359375
LN2_LO = math.log(2.0) - 0.693359375
LOG2E = 1.0 / math.log(2.0)
F32 = jnp.float32
BF16 = jnp.bfloat16
EMPTY = -4000.0
TINY = 1.1754944e-38
N_HALO = 89
N_PACK = 113


def kernel_tables():
    a = np.arange(8)[:, None] + 8
    y = np.arange(24)[None, :]
    k1 = np.exp(-((a - y) ** 2) / 32.0)
    full = np.einsum("ay,bz->yzab", k1, k1).reshape(24, 3, 8, 64)
    full = full.transpose(1, 0, 2, 3)
    hi = full.astype(ml_dtypes.bfloat16)
    lo = (full - hi.astype(np.float64)).astype(ml_dtypes.bfloat16)
    forward = np.concatenate([hi, hi, lo], axis=3).reshape(576, 192)
    hi_rows = hi.reshape(3, 192, 64).transpose(0, 2, 1)
    lo_rows = lo.reshape(3, 192, 64).transpose(0, 2, 1)
    backward = np.concatenate([hi_rows, lo_rows], axis=1)
    return forward, backward


def roll_left(x):
    return pltpu.roll(x, LANES - 1, axis=x.ndim - 1)


def roll_right(x):
    return pltpu.roll(x, 1, axis=x.ndim - 1)


def lanes_of(shape):
    return lax.broadcasted_iota(jnp.int32, shape, len(shape) - 1)


def swap(x, first):
    return jnp.where(first, roll_left(x), roll_right(x))


def up8(x):
    return jnp.broadcast_to(x, (8, LANES))


def halves(x):
    hi = x.astype(BF16)
    lo = (x - hi.astype(F32)).astype(BF16)
    return hi, lo


def spread(u):
    hi, lo = halves(u)
    return jnp.concatenate([hi, lo, hi], axis=0)


def levels(e, ep, first, lam):
    sides = ((0,), (0, 1), (1,))
    ex, sh = [], []
    for part in range(3):
        own = [e[s] for s in sides[part]]
        both = own + [ep[s] for s in sides[part]]
        ex.append(functools.reduce(jnp.maximum, own))
        sh.append(functools.reduce(jnp.maximum, both))
    level = [
        [jnp.where(first, ex[p], sh[p]), sh[p], jnp.where(first, sh[p], ex[p])] for p in range(3)
    ]
    own_w, partner_w = [], []
    for p in range(3):
        own_w.append([[jnp.exp2(e[s] - level[p][b]) for b in range(3)] for s in sides[p]])
        rows = []
        for s in sides[p]:
            raw = [jnp.exp2(ep[s] - level[p][b]) for b in range(3)]
            rows.append([jnp.where(first, 0.0, raw[0]), raw[1], jnp.where(first, raw[2], 0.0)])
        partner_w.append(rows)
    if lam is None:
        new_e = [e[0], e[1]]
        lam_b = [[0.0] * 3 for _ in range(3)]
    else:
        lam_ex, lam_sh, lam_b = lam
        new_e = []
        for s, parts in ((0, (0, 1)), (1, (1, 2))):
            top = functools.reduce(
                jnp.maximum, [lam_ex[p] - ex[p] for p in parts] + [lam_sh[p] - sh[p] for p in parts]
            )
            new_e.append(-top)
    out_w, final_w = [], []
    for s, parts in ((0, (0, 1)), (1, (1, 2))):
        out_w.append(
            {p: [jnp.exp2(lam_b[p][b] - level[p][b] + new_e[s]) for b in range(3)] for p in parts}
        )
        final_w.append(
            {p: [jnp.exp2(e[s] - level[p][b] + lam_b[p][b]) for b in range(3)] for p in parts}
        )
    return own_w, partner_w, out_w, final_w, new_e, level


def region_scale(nu_ref, at, first):
    peak = []
    for part, (y0, y1) in enumerate(((0, 8), (8, 24), (24, 32))):
        row = []
        for b in range(3):
            top = jnp.max(nu_ref[b, y0:y1, :, at], axis=0)
            row.append(up8(jnp.max(top, axis=0, keepdims=True)))
        peak.append(row)

    def lg(x):
        exponent = jnp.floor(jnp.log(jnp.maximum(x, TINY)) * LOG2E)
        return jnp.where(x < TINY, EMPTY, exponent)

    lam_ex = [lg(jnp.where(first, peak[p][0], peak[p][2])) for p in range(3)]
    lam_sh = [
        lg(jnp.maximum(peak[p][1], jnp.where(first, peak[p][2], peak[p][0]))) for p in range(3)
    ]
    lam_b = [
        [
            jnp.where(first, lam_ex[p], lam_sh[p]),
            lam_sh[p],
            jnp.where(first, lam_sh[p], lam_ex[p]),
        ]
        for p in range(3)
    ]
    for part, (y0, y1) in enumerate(((0, 8), (8, 24), (24, 32))):
        for b in range(3):
            nu_ref[b, y0:y1, :, at] = nu_ref[b, y0:y1, :, at] * jnp.exp2(
                -jnp.maximum(lam_b[part][b], -125.0)
            )[None]
    return lam_ex, lam_sh, lam_b


def forward_sums(kf_ref, s_ref, side, u, up):
    cols = []
    for g in range(len(u)):
        cols += [u[g], up[g]]
    out = jnp.dot(
        kf_ref[...], spread(jnp.concatenate(cols, axis=1)), preferred_element_type=F32
    )
    s_ref[side, :, :, :, 0 : out.shape[1]] = out.reshape(3, 24, 8, out.shape[1])


def lanes_at(g):
    return slice(g * LANES, (g + 1) * LANES)


def ratio_rows(s_ref, nu_ref, g, chunk, b, own_w, partner_w, first):
    part = (0, 1, 1, 2)[chunk]
    sides = ((0,), (0, 1), (1,))[part]
    own_at, partner_at = lanes_at(2 * g), lanes_at(2 * g + 1)
    total = None
    for i, s in enumerate(sides):
        y0 = 8 * (chunk - s)
        own = s_ref[s, b, y0 : y0 + 8, :, own_at]
        if b == 1:
            partner = jnp.where(
                first[None],
                s_ref[s, 0, y0 : y0 + 8, :, partner_at],
                s_ref[s, 2, y0 : y0 + 8, :, partner_at],
            )
        else:
            partner = s_ref[s, 1, y0 : y0 + 8, :, partner_at]
        term = own * own_w[part][i][b][None] + partner * partner_w[part][i][b][None]
        total = term if total is None else total + term
    return nu_ref[b, 8 * chunk : 8 * chunk + 8, :, lanes_at(g)] / total


def backward(kb_ref, r_ref, s_ref, nu_ref, groups, weights, first, m):
    width = groups * LANES
    for g in range(groups):
        own_w, partner_w, out_w = weights[g][:3]
        for chunk in range(4):
            part = (0, 1, 1, 2)[chunk]
            for b in range(3):
                r = ratio_rows(s_ref, nu_ref, g, chunk, b, own_w, partner_w, first)
                for s in ((0,), (0, 1), (1,))[part]:
                    y0 = 8 * (chunk - s)
                    at = slice(s * width + g * LANES, s * width + (g + 1) * LANES)
                    r_ref[b, y0 : y0 + 8, :, at] = r * out_w[s][part][b][None]
    total = None
    for b in range(3):
        hi, lo = halves(r_ref[b, 0:24, :, 0 : 2 * width].reshape(192, 2 * width))
        top = jnp.dot(kb_ref[b], hi, preferred_element_type=F32)
        low = jnp.dot(kb_ref[b, 0:64, :], lo, preferred_element_type=F32)
        term = top[0:64] + (top[64:128] + low)
        total = term if total is None else total + term
    out = []
    for s in range(2):
        out.append(
            [
                m[s][g] / total[:, s * width + g * LANES : s * width + (g + 1) * LANES]
                for g in range(groups)
            ]
        )
    return out


def alpha_of(u, e):
    shape = u.shape
    e = jnp.broadcast_to(e[None], (shape[0] // 8, 8, LANES)).reshape(shape)
    return e * LN2_HI + (jnp.log(u) + e * LN2_LO)


def body(
    nx,
    ny,
    mass_ref,
    alpha_ref,
    part_ref,
    kf_ref,
    kb_ref,
    out_alpha_ref,
    out_part_ref,
    pu,
    pm,
    pq,
    pe,
    pack,
    gy_in,
    stage,
    s_ref,
    r_ref,
    nu_ref,
    e_ref,
    send_sem,
    recv_sem,
):
    gx = lax.axis_index("gx")
    gy = lax.axis_index("gy")
    core = lax.rem(gx, 2)
    near = (gx + 1 - 2 * core, gy)
    far = (lax.rem(gx + nx - 1 + 2 * core, nx), gy)
    before = (gx, lax.rem(gy + ny - 1, ny))
    after = (gx, lax.rem(gy + 1, ny))
    barrier = pltpu.get_barrier_semaphore()
    for target in (near, far, before, after):
        pl.semaphore_signal(barrier, inc=1, device_id=target, device_id_type=MESH)

    lane = lanes_of((8, LANES))
    odd = lax.rem(lane, 2) == 1
    even = jnp.logical_not(odd)
    edge = (lane == 0) | (lane == LANES - 1)

    phase_of = [jnp.where(core == c, 1, 0) for c in range(2)]
    u, e, m = [], [], []
    for c in range(2):
        alpha = alpha_ref[c]
        top = jnp.max(jnp.max(alpha, axis=0), axis=0, keepdims=True)
        level = up8(jnp.floor(top * LOG2E))
        u.append([jnp.exp((alpha - level[None] * LN2_HI) - level[None] * LN2_LO).reshape(64, LANES)])
        e.append(level)
        mass = mass_ref[c].reshape(64, LANES)
        m.append([mass])
        pm[phase_of[c], 1 - c] = mass
    for b in range(3):
        z = slice(8 * b, 8 * b + 8)
        for chunk in range(4):
            total = None
            for c in ((0,), (0, 1), (0, 1), (1,))[chunk]:
                y = slice(8 * (chunk - c), 8 * (chunk - c) + 8)
                term = part_ref[c, y, z, :]
                partner = part_ref[c, y, 8:16, :]
                if b == 1:
                    partner = jnp.where(even[None], part_ref[c, y, 0:8, :], part_ref[c, y, 16:24, :])
                total_own = term
                if b == 0:
                    source, mask = part_ref[c, y, 8:16, :], odd
                elif b == 2:
                    source, mask = part_ref[c, y, 8:16, :], even
                else:
                    source = jnp.where(even[None], part_ref[c, y, 16:24, :], part_ref[c, y, 0:8, :])
                    mask = None
                moved = swap(source, even[None])
                if mask is not None:
                    moved = jnp.where(mask[None], moved, 0.0)
                term = total_own + moved
                total = term if total is None else total + term
            nu_ref[b, 8 * chunk : 8 * chunk + 8, :, 0:LANES] = total
    ep = [swap(e[c], even) for c in range(2)]
    weights = [levels(e, ep, even, None)]
    for _ in range(ITERS):
        for c in range(2):
            forward_sums(kf_ref, s_ref, c, u[c], [swap(u[c][0], even[0:1])])
        u = backward(kb_ref, r_ref, s_ref, nu_ref, 1, weights, even, m)
    for c in range(2):
        forward_sums(kf_ref, s_ref, c, u[c], [swap(u[c][0], even[0:1])])
    own_w, partner_w, level = weights[0][0], weights[0][1], weights[0][5]
    for chunk in range(4):
        part = (0, 1, 1, 2)[chunk]
        for b in range(3):
            r = ratio_rows(s_ref, nu_ref, 0, chunk, b, own_w, partner_w, even)
            for c in ((0,), (0, 1), (1,))[part]:
                y0 = 8 * (chunk - c)
                root = jnp.exp2(0.5 * (e[c] - level[part][b]))[None]
                value = (s_ref[c, b, y0 : y0 + 8, :, 0:LANES] * root) * (r * root)
                stage[c, 24 * b + y0 : 24 * b + y0 + 8] = value
    for c in range(2):
        stage[c, 72:80] = u[c][0].reshape(8, 8, LANES)
        stage[c, 80:81] = e[c][None]
        stage[c, 81:89] = m[c][0].reshape(8, 8, LANES)
        low, mid, high = stage[c, 0:24], stage[c, 24:48], stage[c, 48:72]
        stage[c, 89:113] = jnp.where((lane == LANES - 1)[None], high, low)
        pu[phase_of[c], 1 - c, 0:64] = u[c][0]
        pu[phase_of[c], 1 - c, 64:72] = e[c]
        moved = swap(jnp.where(odd[None], high, low), odd[None])
        mid = mid + jnp.where(edge[None], 0.0, moved)
        pq[phase_of[c], 1 - c, 0] = jnp.where(odd[None], low, mid)
        pq[phase_of[c], 1 - c, 1] = jnp.where(odd[None], mid, high)

    def pack_step(i, held):
        out = []
        for c in range(2):
            for half in range(2):
                x = stage[c, half * 64 + i]
                x = pltpu.roll(x, 2 * i + 1, axis=1)
                out.append(jnp.where(lax.div(lane, 2) == i, x, held[2 * c + half]))
        return tuple(out)

    for c in range(2):
        stage[c, 113:128] = jnp.zeros((15, 8, LANES), F32)
    zero = jnp.zeros((8, LANES), F32)
    packed = lax.fori_loop(0, 64, pack_step, (zero, zero, zero, zero))
    for c in range(2):
        for half in range(2):
            pack[c, half] = packed[2 * c + half]

    pl.semaphore_wait(barrier, 4)

    def copy(src, dst, sem, target):
        return pltpu.make_async_remote_copy(
            src_ref=src,
            dst_ref=dst,
            send_sem=send_sem.at[sem],
            recv_sem=recv_sem.at[sem],
            device_id=target,
            device_id_type=MESH,
        )

    near_side, far_side = core, 1 - core
    to_before = copy(pack, gy_in.at[1], 0, before)
    to_after = copy(pack, gy_in.at[0], 1, after)
    to_before.start()
    to_after.start()
    sends = {}
    for name, phase, side, target, sem in (
        ("far", 1, far_side, far, 2),
        ("near", 0, near_side, near, 6),
    ):
        for i, buf in enumerate((pu, pq, pm)):
            where = buf.at[phase, side]
            sends[name, i] = copy(where, where, sem + i, target)
            sends[name, i].start()
        where = pe.at[phase, side]
        sends[name, 3] = copy(where, where, sem + 3, target)
    to_before.wait()
    to_after.wait()
    own_entry = (lane >= 2 * (N_HALO - 64))
    for c in range(2):
        for half in range(2):
            merged = jnp.where(even, gy_in[0, c, half], gy_in[1, c, half])
            if half == 1:
                merged = jnp.where(own_entry, pack[c, half], merged)
            pe[phase_of[c], 1 - c, half] = merged
    sends["near", 3].start()
    sends["far", 3].start()

    for phase, name in ((0, "near"), (1, "far")):
        for i in range(4):
            sends[name, i].wait()
        own_side = near_side if phase == 0 else far_side

        def unpack_step(i, _):
            for side in range(2):
                for half in range(2):
                    shift = LANES - (2 * i + 1)
                    stage[side, half * 64 + i] = pltpu.roll(pe[phase, side, half], shift, axis=1)
            return 0

        lax.fori_loop(0, 64, unpack_step, 0)

        for chunk in range(4):
            sides = ((0,), (0, 1), (0, 1), (1,))[chunk]

            def both(read):
                total = None
                for s in sides:
                    term = read(s, 8 * (chunk - s))
                    total = term if total is None else total + term
                return total

            low = both(lambda s, y: pq[phase, s, 0, y : y + 8])
            high = both(lambda s, y: pq[phase, s, 1, y : y + 8])
            ep0, ep1, ep2 = [
                both(lambda s, y, b=b: stage[s, 24 * b + y : 24 * b + y + 8]) for b in range(3)
            ]
            kept = both(lambda s, y: stage[s, 89 + y : 89 + y + 8])
            moved = swap(jnp.where(odd[None], ep2, ep0), odd[None])
            low = low + jnp.where((lane == 0)[None], moved, 0.0)
            high = high + jnp.where((lane == LANES - 1)[None], moved, 0.0)
            other = swap(jnp.where(odd[None], high, low), odd[None])
            other = jnp.where(edge[None], kept + swap(ep1, odd[None]), other)
            rows = slice(8 * chunk, 8 * chunk + 8)
            main, outer = lanes_at(0), lanes_at(1)
            nu_ref[0, rows, :, main] = jnp.where(odd[None], low, other)
            nu_ref[1, rows, :, main] = jnp.where(odd[None], high, low)
            nu_ref[2, rows, :, main] = jnp.where(odd[None], other, high)
            nu_ref[0, rows, :, outer] = jnp.where(odd[None], ep0, swap(high, odd[None]))
            nu_ref[1, rows, :, outer] = swap(other, odd[None])
            nu_ref[2, rows, :, outer] = jnp.where(odd[None], swap(low, odd[None]), ep2)

        u = [[pu[phase, s, 0:64], stage[s, 72:80].reshape(64, LANES)] for s in range(2)]
        e = [[pu[phase, s, 64:72], stage[s, 80]] for s in range(2)]
        m = [[pm[phase, s], stage[s, 81:89].reshape(64, LANES)] for s in range(2)]
        lam = [region_scale(nu_ref, lanes_at(g), odd) for g in range(2)]

        def partners(x, mask, at_edge):
            moved_main, moved_edge = swap(x[0], mask), swap(x[1], mask)
            return [jnp.where(at_edge, moved_edge, moved_main), moved_main]

        for it in range(ITERS + 1):
            for s in range(2):
                forward_sums(kf_ref, s_ref, s, u[s], partners(u[s], odd[0:1], edge[0:1]))
            ep = [partners(e[s], odd, edge) for s in range(2)]
            weights = [
                levels([e[0][g], e[1][g]], [ep[0][g], ep[1][g]], odd, lam[g]) for g in range(2)
            ]
            if it < ITERS:
                u = backward(kb_ref, r_ref, s_ref, nu_ref, 2, weights, odd, m)
                e = [[weights[g][4][s] for g in range(2)] for s in range(2)]

        own_w, partner_w, _, final_w = weights[0][:4]
        own_col = 1 - own_side
        for chunk in range(4):
            for b in range(3):
                r_ref[b, 8 * chunk : 8 * chunk + 8, :, 0:LANES] = ratio_rows(
                    s_ref, nu_ref, 0, chunk, b, own_w, partner_w, odd
                )
        for b in range(3):
            e_ref[0, b] = final_w[0][0][b]
            e_ref[1, b] = final_w[0][1][b]
            e_ref[2, b] = final_w[0][1][b]
            e_ref[3, b] = final_w[1][1][b]
            e_ref[4, b] = final_w[1][1][b]
            e_ref[5, b] = final_w[1][2][b]
        for k in range(3):
            for b in range(3):
                r = r_ref[b, pl.ds(8 * (k + own_side), 8), :, 0:LANES]
                scale = e_ref[3 * own_side + k, b]
                sums = s_ref[own_side, b, 8 * k : 8 * k + 8, :, 0:LANES]
                out_part_ref[own_col, 8 * k : 8 * k + 8, 8 * b : 8 * b + 8, :] = sums * (
                    r * scale[None]
                )
        left = (own_side == 0)
        own_u = jnp.where(left, u[0][0], u[1][0])
        own_e = jnp.where(left, e[0][0], e[1][0])
        out_alpha_ref[own_col] = alpha_of(own_u, own_e).reshape(8, 8, LANES)


def per_device(nx, ny, source_mass, alpha_start, part_start):
    forward, back = kernel_tables()
    vmem = pl.BlockSpec(memory_space=pltpu.VMEM)
    return pl.pallas_call(
        functools.partial(body, nx, ny),
        out_shape=(
            jax.ShapeDtypeStruct(alpha_start.shape, F32),
            jax.ShapeDtypeStruct(part_start.shape, F32),
        ),
        in_specs=[vmem] * 5,
        out_specs=(vmem, vmem),
        scratch_shapes=[
            pltpu.VMEM((2, 2, 72, LANES), F32),
            pltpu.VMEM((2, 2, 64, LANES), F32),
            pltpu.VMEM((2, 2, 2, 24, 8, LANES), F32),
            pltpu.VMEM((2, 2, 2, 8, LANES), F32),
            pltpu.VMEM((2, 2, 8, LANES), F32),
            pltpu.VMEM((2, 2, 2, 8, LANES), F32),
            pltpu.VMEM((2, 128, 8, LANES), F32),
            pltpu.VMEM((2, 3, 24, 8, 4 * LANES), F32),
            pltpu.VMEM((3, 32, 8, 4 * LANES), F32),
            pltpu.VMEM((3, 32, 8, 2 * LANES), F32),
            pltpu.VMEM((6, 3, 8, LANES), F32),
            pltpu.SemaphoreType.DMA((10,)),
            pltpu.SemaphoreType.DMA((10,)),
        ],
        compiler_params=pltpu.CompilerParams(
            collective_id=0, has_side_effects=True, vmem_limit_bytes=48 * 2**20
        ),
    )(source_mass, alpha_start, part_start, jnp.asarray(forward), jnp.asarray(back))


def solution(mesh):
    placed = P("gx", None, None, "gy")
    return jax.shard_map(
        functools.partial(per_device, mesh.shape["gx"], mesh.shape["gy"]),
        mesh=mesh,
        in_specs=(placed, placed, placed),
        out_specs=(placed, placed),
        check_vma=False,
    )
```

```python
import functools
import math

import jax
import jax.numpy as jnp
import ml_dtypes
import numpy as np
from jax import lax
from jax.experimental import pallas as pl
from jax.experimental.pallas import tpu as pltpu
from jax.sharding import PartitionSpec as P

ITERS = 2
LANES = 128
MESH = pl.DeviceIdType.MESH
LN2_HI = 0.693359375
LN2_LO = math.log(2.0) - 0.693359375
LOG2E = 1.0 / math.log(2.0)
F32 = jnp.float32
BF16 = jnp.bfloat16
EMPTY = -4000.0
TINY = 1.1754944e-38
N_HALO = 89
N_PACK = 113


def kernel_tables():
    a = np.arange(8)[:, None] + 8
    y = np.arange(24)[None, :]
    k1 = np.exp(-((a - y) ** 2) / 32.0)
    full = np.einsum("ay,bz->yzab", k1, k1).reshape(24, 3, 8, 64)
    full = full.transpose(1, 0, 2, 3)
    hi = full.astype(ml_dtypes.bfloat16)
    lo = (full - hi.astype(np.float64)).astype(ml_dtypes.bfloat16)
    forward = np.concatenate([hi, hi, lo], axis=3).reshape(576, 192)
    hi_rows = hi.reshape(3, 192, 64).transpose(0, 2, 1)
    lo_rows = lo.reshape(3, 192, 64).transpose(0, 2, 1)
    backward = np.concatenate([hi_rows, lo_rows], axis=1)
    return forward, backward


def roll_left(x):
    return pltpu.roll(x, LANES - 1, axis=x.ndim - 1)


def roll_right(x):
    return pltpu.roll(x, 1, axis=x.ndim - 1)


def lanes_of(shape):
    return lax.broadcasted_iota(jnp.int32, shape, len(shape) - 1)


def swap(x, first):
    return jnp.where(first, roll_left(x), roll_right(x))


def up8(x):
    return jnp.broadcast_to(x, (8, LANES))


def halves(x):
    hi = x.astype(BF16)
    lo = (x - hi.astype(F32)).astype(BF16)
    return hi, lo


def spread(u):
    hi, lo = halves(u)
    return jnp.concatenate([hi, lo, hi], axis=0)


def levels(e, ep, first, lam):
    sides = ((0,), (0, 1), (1,))
    ex, sh = [], []
    for part in range(3):
        own = [e[s] for s in sides[part]]
        both = own + [ep[s] for s in sides[part]]
        ex.append(functools.reduce(jnp.maximum, own))
        sh.append(functools.reduce(jnp.maximum, both))
    level = [
        [jnp.where(first, ex[p], sh[p]), sh[p], jnp.where(first, sh[p], ex[p])] for p in range(3)
    ]
    own_w, partner_w = [], []
    for p in range(3):
        own_w.append([[jnp.exp2(e[s] - level[p][b]) for b in range(3)] for s in sides[p]])
        rows = []
        for s in sides[p]:
            raw = [jnp.exp2(ep[s] - level[p][b]) for b in range(3)]
            rows.append([jnp.where(first, 0.0, raw[0]), raw[1], jnp.where(first, raw[2], 0.0)])
        partner_w.append(rows)
    if lam is None:
        new_e = [e[0], e[1]]
        lam_b = [[0.0] * 3 for _ in range(3)]
    else:
        lam_ex, lam_sh, lam_b = lam
        new_e = []
        for s, parts in ((0, (0, 1)), (1, (1, 2))):
            top = functools.reduce(
                jnp.maximum, [lam_ex[p] - ex[p] for p in parts] + [lam_sh[p] - sh[p] for p in parts]
            )
            new_e.append(-top)
    out_w, final_w = [], []
    for s, parts in ((0, (0, 1)), (1, (1, 2))):
        out_w.append(
            {p: [jnp.exp2(lam_b[p][b] - level[p][b] + new_e[s]) for b in range(3)] for p in parts}
        )
        final_w.append(
            {p: [jnp.exp2(e[s] - level[p][b] + lam_b[p][b]) for b in range(3)] for p in parts}
        )
    return own_w, partner_w, out_w, final_w, new_e, level


def region_scale(nu_ref, at, first):
    peak = []
    for part, (y0, y1) in enumerate(((0, 8), (8, 24), (24, 32))):
        row = []
        for b in range(3):
            top = jnp.max(nu_ref[b, y0:y1, :, at], axis=0)
            row.append(up8(jnp.max(top, axis=0, keepdims=True)))
        peak.append(row)

    def lg(x):
        exponent = jnp.floor(jnp.log(jnp.maximum(x, TINY)) * LOG2E)
        return jnp.where(x < TINY, EMPTY, exponent)

    lam_ex = [lg(jnp.where(first, peak[p][0], peak[p][2])) for p in range(3)]
    lam_sh = [
        lg(jnp.maximum(peak[p][1], jnp.where(first, peak[p][2], peak[p][0]))) for p in range(3)
    ]
    lam_b = [
        [
            jnp.where(first, lam_ex[p], lam_sh[p]),
            lam_sh[p],
            jnp.where(first, lam_sh[p], lam_ex[p]),
        ]
        for p in range(3)
    ]
    for part, (y0, y1) in enumerate(((0, 8), (8, 24), (24, 32))):
        for b in range(3):
            nu_ref[b, y0:y1, :, at] = nu_ref[b, y0:y1, :, at] * jnp.exp2(
                -jnp.maximum(lam_b[part][b], -125.0)
            )[None]
    return lam_ex, lam_sh, lam_b


def forward_sums(kf_ref, s_ref, side, u, up):
    cols = []
    for g in range(len(u)):
        cols += [u[g], up[g]]
    out = jnp.dot(
        kf_ref[...], spread(jnp.concatenate(cols, axis=1)), preferred_element_type=F32
    )
    s_ref[side, :, :, :, 0 : out.shape[1]] = out.reshape(3, 24, 8, out.shape[1])


def lanes_at(g):
    return slice(g * LANES, (g + 1) * LANES)


def ratio_rows(s_ref, nu_ref, g, chunk, b, own_w, partner_w, first):
    part = (0, 1, 1, 2)[chunk]
    sides = ((0,), (0, 1), (1,))[part]
    own_at, partner_at = lanes_at(2 * g), lanes_at(2 * g + 1)
    total = None
    for i, s in enumerate(sides):
        y0 = 8 * (chunk - s)
        own = s_ref[s, b, y0 : y0 + 8, :, own_at]
        if b == 1:
            partner = jnp.where(
                first[None],
                s_ref[s, 0, y0 : y0 + 8, :, partner_at],
                s_ref[s, 2, y0 : y0 + 8, :, partner_at],
            )
        else:
            partner = s_ref[s, 1, y0 : y0 + 8, :, partner_at]
        term = own * own_w[part][i][b][None] + partner * partner_w[part][i][b][None]
        total = term if total is None else total + term
    return nu_ref[b, 8 * chunk : 8 * chunk + 8, :, lanes_at(g)] / total


def backward(kb_ref, r_ref, s_ref, nu_ref, groups, weights, first, m):
    width = groups * LANES
    for g in range(groups):
        own_w, partner_w, out_w = weights[g][:3]
        for chunk in range(4):
            part = (0, 1, 1, 2)[chunk]
            for b in range(3):
                r = ratio_rows(s_ref, nu_ref, g, chunk, b, own_w, partner_w, first)
                for s in ((0,), (0, 1), (1,))[part]:
                    y0 = 8 * (chunk - s)
                    at = slice(s * width + g * LANES, s * width + (g + 1) * LANES)
                    r_ref[b, y0 : y0 + 8, :, at] = r * out_w[s][part][b][None]
    total = None
    for b in range(3):
        hi, lo = halves(r_ref[b, 0:24, :, 0 : 2 * width].reshape(192, 2 * width))
        top = jnp.dot(kb_ref[b], hi, preferred_element_type=F32)
        low = jnp.dot(kb_ref[b, 0:64, :], lo, preferred_element_type=F32)
        term = top[0:64] + (top[64:128] + low)
        total = term if total is None else total + term
    out = []
    for s in range(2):
        out.append(
            [
                m[s][g] / total[:, s * width + g * LANES : s * width + (g + 1) * LANES]
                for g in range(groups)
            ]
        )
    return out


def alpha_of(u, e):
    shape = u.shape
    e = jnp.broadcast_to(e[None], (shape[0] // 8, 8, LANES)).reshape(shape)
    return e * LN2_HI + (jnp.log(u) + e * LN2_LO)


def body(
    nx,
    ny,
    mass_hbm,
    alpha_hbm,
    part_hbm,
    kf_hbm,
    kb_hbm,
    out_alpha_ref,
    out_part_ref,
    pu,
    pm,
    pq,
    pe,
    pack,
    gy_in,
    stage,
    s_ref,
    r_ref,
    nu_ref,
    e_ref,
    mass_ref,
    alpha_ref,
    part_ref,
    kf_ref,
    kb_ref,
    load_sem,
    send_sem,
    recv_sem,
):
    gx = lax.axis_index("gx")
    gy = lax.axis_index("gy")
    core = lax.rem(gx, 2)
    near = (gx + 1 - 2 * core, gy)
    far = (lax.rem(gx + nx - 1 + 2 * core, nx), gy)
    before = (gx, lax.rem(gy + ny - 1, ny))
    after = (gx, lax.rem(gy + 1, ny))
    barrier = pltpu.get_barrier_semaphore()
    for target in (near, far, before, after):
        pl.semaphore_signal(barrier, inc=1, device_id=target, device_id_type=MESH)

    loads = [
        pltpu.make_async_copy(src, dst, load_sem.at[i])
        for i, (src, dst) in enumerate(
            (
                (alpha_hbm, alpha_ref),
                (mass_hbm, mass_ref),
                (part_hbm, part_ref),
                (kf_hbm, kf_ref),
                (kb_hbm, kb_ref),
            )
        )
    ]
    for load in loads:
        load.start()

    lane = lanes_of((8, LANES))
    odd = lax.rem(lane, 2) == 1
    even = jnp.logical_not(odd)
    edge = (lane == 0) | (lane == LANES - 1)

    phase_of = [jnp.where(core == c, 1, 0) for c in range(2)]
    u, e, m = [], [], []
    loads[0].wait()
    loads[1].wait()
    for c in range(2):
        alpha = alpha_ref[c]
        top = jnp.max(jnp.max(alpha, axis=0), axis=0, keepdims=True)
        level = up8(jnp.floor(top * LOG2E))
        u.append([jnp.exp((alpha - level[None] * LN2_HI) - level[None] * LN2_LO).reshape(64, LANES)])
        e.append(level)
        mass = mass_ref[c].reshape(64, LANES)
        m.append([mass])
        pm[phase_of[c], 1 - c] = mass
    loads[2].wait()
    for b in range(3):
        z = slice(8 * b, 8 * b + 8)
        for chunk in range(4):
            total = None
            for c in ((0,), (0, 1), (0, 1), (1,))[chunk]:
                y = slice(8 * (chunk - c), 8 * (chunk - c) + 8)
                term = part_ref[c, y, z, :]
                partner = part_ref[c, y, 8:16, :]
                if b == 1:
                    partner = jnp.where(even[None], part_ref[c, y, 0:8, :], part_ref[c, y, 16:24, :])
                total_own = term
                if b == 0:
                    source, mask = part_ref[c, y, 8:16, :], odd
                elif b == 2:
                    source, mask = part_ref[c, y, 8:16, :], even
                else:
                    source = jnp.where(even[None], part_ref[c, y, 16:24, :], part_ref[c, y, 0:8, :])
                    mask = None
                moved = swap(source, even[None])
                if mask is not None:
                    moved = jnp.where(mask[None], moved, 0.0)
                term = total_own + moved
                total = term if total is None else total + term
            nu_ref[b, 8 * chunk : 8 * chunk + 8, :, 0:LANES] = total
    ep = [swap(e[c], even) for c in range(2)]
    weights = [levels(e, ep, even, None)]
    loads[3].wait()
    loads[4].wait()
    for _ in range(ITERS):
        for c in range(2):
            forward_sums(kf_ref, s_ref, c, u[c], [swap(u[c][0], even[0:1])])
        u = backward(kb_ref, r_ref, s_ref, nu_ref, 1, weights, even, m)
    for c in range(2):
        forward_sums(kf_ref, s_ref, c, u[c], [swap(u[c][0], even[0:1])])
    own_w, partner_w, level = weights[0][0], weights[0][1], weights[0][5]
    for chunk in range(4):
        part = (0, 1, 1, 2)[chunk]
        for b in range(3):
            r = ratio_rows(s_ref, nu_ref, 0, chunk, b, own_w, partner_w, even)
            for c in ((0,), (0, 1), (1,))[part]:
                y0 = 8 * (chunk - c)
                root = jnp.exp2(0.5 * (e[c] - level[part][b]))[None]
                value = (s_ref[c, b, y0 : y0 + 8, :, 0:LANES] * root) * (r * root)
                stage[c, 24 * b + y0 : 24 * b + y0 + 8] = value
    for c in range(2):
        stage[c, 72:80] = u[c][0].reshape(8, 8, LANES)
        stage[c, 80:81] = e[c][None]
        stage[c, 81:89] = m[c][0].reshape(8, 8, LANES)
        low, mid, high = stage[c, 0:24], stage[c, 24:48], stage[c, 48:72]
        stage[c, 89:113] = jnp.where((lane == LANES - 1)[None], high, low)
        pu[phase_of[c], 1 - c, 0:64] = u[c][0]
        pu[phase_of[c], 1 - c, 64:72] = e[c]
        moved = swap(jnp.where(odd[None], high, low), odd[None])
        mid = mid + jnp.where(edge[None], 0.0, moved)
        pq[phase_of[c], 1 - c, 0] = jnp.where(odd[None], low, mid)
        pq[phase_of[c], 1 - c, 1] = jnp.where(odd[None], mid, high)

    def pack_step(i, held):
        out = []
        for c in range(2):
            for half in range(2):
                x = stage[c, half * 64 + i]
                x = pltpu.roll(x, 2 * i + 1, axis=1)
                out.append(jnp.where(lax.div(lane, 2) == i, x, held[2 * c + half]))
        return tuple(out)

    for c in range(2):
        stage[c, 113:128] = jnp.zeros((15, 8, LANES), F32)
    zero = jnp.zeros((8, LANES), F32)
    packed = lax.fori_loop(0, 64, pack_step, (zero, zero, zero, zero), unroll=16)
    for c in range(2):
        for half in range(2):
            pack[c, half] = packed[2 * c + half]

    pl.semaphore_wait(barrier, 4)

    def copy(src, dst, sem, target):
        return pltpu.make_async_remote_copy(
            src_ref=src,
            dst_ref=dst,
            send_sem=send_sem.at[sem],
            recv_sem=recv_sem.at[sem],
            device_id=target,
            device_id_type=MESH,
        )

    near_side, far_side = core, 1 - core
    to_before = copy(pack, gy_in.at[1], 0, before)
    to_after = copy(pack, gy_in.at[0], 1, after)
    to_before.start()
    to_after.start()
    sends = {}
    for name, phase, side, target, sem in (
        ("far", 1, far_side, far, 2),
        ("near", 0, near_side, near, 6),
    ):
        for i, buf in enumerate((pu, pq, pm)):
            where = buf.at[phase, side]
            sends[name, i] = copy(where, where, sem + i, target)
            sends[name, i].start()
        where = pe.at[phase, side]
        sends[name, 3] = copy(where, where, sem + 3, target)
    to_before.wait()
    to_after.wait()
    own_entry = (lane >= 2 * (N_HALO - 64))
    for c in range(2):
        for half in range(2):
            merged = jnp.where(even, gy_in[0, c, half], gy_in[1, c, half])
            if half == 1:
                merged = jnp.where(own_entry, pack[c, half], merged)
            pe[phase_of[c], 1 - c, half] = merged
    sends["near", 3].start()
    sends["far", 3].start()

    for phase, name in ((0, "near"), (1, "far")):
        for i in range(4):
            sends[name, i].wait()
        own_side = near_side if phase == 0 else far_side

        def unpack_step(i, _):
            for side in range(2):
                for half in range(2):
                    shift = LANES - (2 * i + 1)
                    stage[side, half * 64 + i] = pltpu.roll(pe[phase, side, half], shift, axis=1)
            return 0

        lax.fori_loop(0, 64, unpack_step, 0, unroll=16)

        for chunk in range(4):
            sides = ((0,), (0, 1), (0, 1), (1,))[chunk]

            def both(read):
                total = None
                for s in sides:
                    term = read(s, 8 * (chunk - s))
                    total = term if total is None else total + term
                return total

            low = both(lambda s, y: pq[phase, s, 0, y : y + 8])
            high = both(lambda s, y: pq[phase, s, 1, y : y + 8])
            ep0, ep1, ep2 = [
                both(lambda s, y, b=b: stage[s, 24 * b + y : 24 * b + y + 8]) for b in range(3)
            ]
            kept = both(lambda s, y: stage[s, 89 + y : 89 + y + 8])
            moved = swap(jnp.where(odd[None], ep2, ep0), odd[None])
            low = low + jnp.where((lane == 0)[None], moved, 0.0)
            high = high + jnp.where((lane == LANES - 1)[None], moved, 0.0)
            other = swap(jnp.where(odd[None], high, low), odd[None])
            other = jnp.where(edge[None], kept + swap(ep1, odd[None]), other)
            rows = slice(8 * chunk, 8 * chunk + 8)
            main, outer = lanes_at(0), lanes_at(1)
            nu_ref[0, rows, :, main] = jnp.where(odd[None], low, other)
            nu_ref[1, rows, :, main] = jnp.where(odd[None], high, low)
            nu_ref[2, rows, :, main] = jnp.where(odd[None], other, high)
            nu_ref[0, rows, :, outer] = jnp.where(odd[None], ep0, swap(high, odd[None]))
            nu_ref[1, rows, :, outer] = swap(other, odd[None])
            nu_ref[2, rows, :, outer] = jnp.where(odd[None], swap(low, odd[None]), ep2)

        u = [[pu[phase, s, 0:64], stage[s, 72:80].reshape(64, LANES)] for s in range(2)]
        e = [[pu[phase, s, 64:72], stage[s, 80]] for s in range(2)]
        m = [[pm[phase, s], stage[s, 81:89].reshape(64, LANES)] for s in range(2)]
        lam = [region_scale(nu_ref, lanes_at(g), odd) for g in range(2)]

        def partners(x, mask, at_edge):
            moved_main, moved_edge = swap(x[0], mask), swap(x[1], mask)
            return [jnp.where(at_edge, moved_edge, moved_main), moved_main]

        for it in range(ITERS + 1):
            for s in range(2):
                forward_sums(kf_ref, s_ref, s, u[s], partners(u[s], odd[0:1], edge[0:1]))
            ep = [partners(e[s], odd, edge) for s in range(2)]
            weights = [
                levels([e[0][g], e[1][g]], [ep[0][g], ep[1][g]], odd, lam[g]) for g in range(2)
            ]
            if it < ITERS:
                u = backward(kb_ref, r_ref, s_ref, nu_ref, 2, weights, odd, m)
                e = [[weights[g][4][s] for g in range(2)] for s in range(2)]

        own_w, partner_w, _, final_w = weights[0][:4]
        own_col = 1 - own_side
        for chunk in range(4):
            for b in range(3):
                r_ref[b, 8 * chunk : 8 * chunk + 8, :, 0:LANES] = ratio_rows(
                    s_ref, nu_ref, 0, chunk, b, own_w, partner_w, odd
                )
        for b in range(3):
            e_ref[0, b] = final_w[0][0][b]
            e_ref[1, b] = final_w[0][1][b]
            e_ref[2, b] = final_w[0][1][b]
            e_ref[3, b] = final_w[1][1][b]
            e_ref[4, b] = final_w[1][1][b]
            e_ref[5, b] = final_w[1][2][b]
        for k in range(3):
            for b in range(3):
                r = r_ref[b, pl.ds(8 * (k + own_side), 8), :, 0:LANES]
                scale = e_ref[3 * own_side + k, b]
                sums = s_ref[own_side, b, 8 * k : 8 * k + 8, :, 0:LANES]
                out_part_ref[own_col, 8 * k : 8 * k + 8, 8 * b : 8 * b + 8, :] = sums * (
                    r * scale[None]
                )
        left = (own_side == 0)
        own_u = jnp.where(left, u[0][0], u[1][0])
        own_e = jnp.where(left, e[0][0], e[1][0])
        out_alpha_ref[own_col] = alpha_of(own_u, own_e).reshape(8, 8, LANES)


def per_device(nx, ny, source_mass, alpha_start, part_start):
    forward, back = kernel_tables()
    vmem = pl.BlockSpec(memory_space=pltpu.VMEM)
    return pl.pallas_call(
        functools.partial(body, nx, ny),
        out_shape=(
            jax.ShapeDtypeStruct(alpha_start.shape, F32),
            jax.ShapeDtypeStruct(part_start.shape, F32),
        ),
        in_specs=[pl.BlockSpec(memory_space=pl.ANY)] * 5,
        out_specs=(vmem, vmem),
        scratch_shapes=[
            pltpu.VMEM((2, 2, 72, LANES), F32),
            pltpu.VMEM((2, 2, 64, LANES), F32),
            pltpu.VMEM((2, 2, 2, 24, 8, LANES), F32),
            pltpu.VMEM((2, 2, 2, 8, LANES), F32),
            pltpu.VMEM((2, 2, 8, LANES), F32),
            pltpu.VMEM((2, 2, 2, 8, LANES), F32),
            pltpu.VMEM((2, 128, 8, LANES), F32),
            pltpu.VMEM((2, 3, 24, 8, 4 * LANES), F32),
            pltpu.VMEM((3, 32, 8, 4 * LANES), F32),
            pltpu.VMEM((3, 32, 8, 2 * LANES), F32),
            pltpu.VMEM((6, 3, 8, LANES), F32),
            pltpu.VMEM(source_mass.shape, F32),
            pltpu.VMEM(alpha_start.shape, F32),
            pltpu.VMEM(part_start.shape, F32),
            pltpu.VMEM(forward.shape, BF16),
            pltpu.VMEM(back.shape, BF16),
            pltpu.SemaphoreType.DMA((5,)),
            pltpu.SemaphoreType.DMA((10,)),
            pltpu.SemaphoreType.DMA((10,)),
        ],
        compiler_params=pltpu.CompilerParams(
            collective_id=0, has_side_effects=True, vmem_limit_bytes=48 * 2**20
        ),
    )(source_mass, alpha_start, part_start, jnp.asarray(forward), jnp.asarray(back))


def solution(mesh):
    placed = P("gx", None, None, "gy")
    return jax.shard_map(
        functools.partial(per_device, mesh.shape["gx"], mesh.shape["gy"]),
        mesh=mesh,
        in_specs=(placed, placed, placed),
        out_specs=(placed, placed),
        check_vma=False,
    )
```

```python
import functools
import math

import jax
import jax.numpy as jnp
import ml_dtypes
import numpy as np
from jax import lax
from jax.experimental import pallas as pl
from jax.experimental.pallas import tpu as pltpu
from jax.sharding import PartitionSpec as P

ITERS = 2
LANES = 128
MESH = pl.DeviceIdType.MESH
LN2_HI = 0.693359375
LN2_LO = math.log(2.0) - 0.693359375
LOG2E = 1.0 / math.log(2.0)
F32 = jnp.float32
BF16 = jnp.bfloat16
EMPTY = -4000.0
TINY = 1.1754944e-38
N_HALO = 89
N_PACK = 113


def kernel_tables():
    a = np.arange(8)[:, None] + 8
    y = np.arange(24)[None, :]
    k1 = np.exp(-((a - y) ** 2) / 32.0)
    full = np.einsum("ay,bz->yzab", k1, k1).reshape(24, 3, 8, 64)
    full = full.transpose(1, 0, 2, 3)
    hi = full.astype(ml_dtypes.bfloat16)
    lo = (full - hi.astype(np.float64)).astype(ml_dtypes.bfloat16)
    forward = np.concatenate([hi, hi, lo], axis=3).reshape(576, 192)
    hi_rows = hi.reshape(3, 192, 64).transpose(0, 2, 1)
    lo_rows = lo.reshape(3, 192, 64).transpose(0, 2, 1)
    backward = np.concatenate([hi_rows, lo_rows], axis=1)
    return forward, backward


def roll_left(x):
    return pltpu.roll(x, LANES - 1, axis=x.ndim - 1)


def roll_right(x):
    return pltpu.roll(x, 1, axis=x.ndim - 1)


def lanes_of(shape):
    return lax.broadcasted_iota(jnp.int32, shape, len(shape) - 1)


def swap(x, first):
    return jnp.where(first, roll_left(x), roll_right(x))


def up8(x):
    return jnp.broadcast_to(x, (8, LANES))


def halves(x):
    hi = x.astype(BF16)
    lo = (x - hi.astype(F32)).astype(BF16)
    return hi, lo


def spread(u):
    hi, lo = halves(u)
    return jnp.concatenate([hi, lo, hi], axis=0)


def levels(e, ep, first, lam):
    sides = ((0,), (0, 1), (1,))
    ex, sh = [], []
    for part in range(3):
        own = [e[s] for s in sides[part]]
        both = own + [ep[s] for s in sides[part]]
        ex.append(functools.reduce(jnp.maximum, own))
        sh.append(functools.reduce(jnp.maximum, both))
    level = [
        [jnp.where(first, ex[p], sh[p]), sh[p], jnp.where(first, sh[p], ex[p])] for p in range(3)
    ]
    own_w, partner_w = [], []
    for p in range(3):
        own_w.append([[jnp.exp2(e[s] - level[p][b]) for b in range(3)] for s in sides[p]])
        rows = []
        for s in sides[p]:
            raw = [jnp.exp2(ep[s] - level[p][b]) for b in range(3)]
            rows.append([jnp.where(first, 0.0, raw[0]), raw[1], jnp.where(first, raw[2], 0.0)])
        partner_w.append(rows)
    if lam is None:
        new_e = [e[0], e[1]]
        lam_b = [[0.0] * 3 for _ in range(3)]
    else:
        lam_ex, lam_sh, lam_b = lam
        new_e = []
        for s, parts in ((0, (0, 1)), (1, (1, 2))):
            top = functools.reduce(
                jnp.maximum, [lam_ex[p] - ex[p] for p in parts] + [lam_sh[p] - sh[p] for p in parts]
            )
            new_e.append(-top)
    out_w, final_w = [], []
    for s, parts in ((0, (0, 1)), (1, (1, 2))):
        out_w.append(
            {p: [jnp.exp2(lam_b[p][b] - level[p][b] + new_e[s]) for b in range(3)] for p in parts}
        )
        final_w.append(
            {p: [jnp.exp2(e[s] - level[p][b] + lam_b[p][b]) for b in range(3)] for p in parts}
        )
    return own_w, partner_w, out_w, final_w, new_e, level


def region_scale(nu_ref, at, first):
    peak = []
    for part, (y0, y1) in enumerate(((0, 8), (8, 24), (24, 32))):
        row = []
        for b in range(3):
            top = jnp.max(nu_ref[b, y0:y1, :, at], axis=0)
            row.append(up8(jnp.max(top, axis=0, keepdims=True)))
        peak.append(row)

    def lg(x):
        exponent = jnp.floor(jnp.log(jnp.maximum(x, TINY)) * LOG2E)
        return jnp.where(x < TINY, EMPTY, exponent)

    lam_ex = [lg(jnp.where(first, peak[p][0], peak[p][2])) for p in range(3)]
    lam_sh = [
        lg(jnp.maximum(peak[p][1], jnp.where(first, peak[p][2], peak[p][0]))) for p in range(3)
    ]
    lam_b = [
        [
            jnp.where(first, lam_ex[p], lam_sh[p]),
            lam_sh[p],
            jnp.where(first, lam_sh[p], lam_ex[p]),
        ]
        for p in range(3)
    ]
    for part, (y0, y1) in enumerate(((0, 8), (8, 24), (24, 32))):
        for b in range(3):
            nu_ref[b, y0:y1, :, at] = nu_ref[b, y0:y1, :, at] * jnp.exp2(
                -jnp.maximum(lam_b[part][b], -125.0)
            )[None]
    return lam_ex, lam_sh, lam_b


def forward_sums(kf_ref, s_ref, side, u, up):
    cols = []
    for g in range(len(u)):
        cols += [u[g], up[g]]
    out = jnp.dot(
        kf_ref[...], spread(jnp.concatenate(cols, axis=1)), preferred_element_type=F32
    )
    s_ref[side, :, :, :, 0 : out.shape[1]] = out.reshape(3, 24, 8, out.shape[1])


def lanes_at(g):
    return slice(g * LANES, (g + 1) * LANES)


def ratio_rows(s_ref, nu_ref, g, chunk, b, own_w, partner_w, first):
    part = (0, 1, 1, 2)[chunk]
    sides = ((0,), (0, 1), (1,))[part]
    own_at, partner_at = lanes_at(2 * g), lanes_at(2 * g + 1)
    total = None
    for i, s in enumerate(sides):
        y0 = 8 * (chunk - s)
        own = s_ref[s, b, y0 : y0 + 8, :, own_at]
        if b == 1:
            partner = jnp.where(
                first[None],
                s_ref[s, 0, y0 : y0 + 8, :, partner_at],
                s_ref[s, 2, y0 : y0 + 8, :, partner_at],
            )
        else:
            partner = s_ref[s, 1, y0 : y0 + 8, :, partner_at]
        term = own * own_w[part][i][b][None] + partner * partner_w[part][i][b][None]
        total = term if total is None else total + term
    return nu_ref[b, 8 * chunk : 8 * chunk + 8, :, lanes_at(g)] / total


def backward(kb_ref, r_ref, s_ref, nu_ref, groups, weights, first, m):
    width = groups * LANES
    for g in range(groups):
        own_w, partner_w, out_w = weights[g][:3]
        for chunk in range(4):
            part = (0, 1, 1, 2)[chunk]
            for b in range(3):
                r = ratio_rows(s_ref, nu_ref, g, chunk, b, own_w, partner_w, first)
                for s in ((0,), (0, 1), (1,))[part]:
                    y0 = 8 * (chunk - s)
                    at = slice(s * width + g * LANES, s * width + (g + 1) * LANES)
                    r_ref[b, y0 : y0 + 8, :, at] = r * out_w[s][part][b][None]
    total = None
    for b in range(3):
        hi, lo = halves(r_ref[b, 0:24, :, 0 : 2 * width].reshape(192, 2 * width))
        top = jnp.dot(kb_ref[b], hi, preferred_element_type=F32)
        low = jnp.dot(kb_ref[b, 0:64, :], lo, preferred_element_type=F32)
        term = top[0:64] + (top[64:128] + low)
        total = term if total is None else total + term
    out = []
    for s in range(2):
        out.append(
            [
                m[s][g] / total[:, s * width + g * LANES : s * width + (g + 1) * LANES]
                for g in range(groups)
            ]
        )
    return out


def alpha_of(u, e):
    shape = u.shape
    e = jnp.broadcast_to(e[None], (shape[0] // 8, 8, LANES)).reshape(shape)
    return e * LN2_HI + (jnp.log(u) + e * LN2_LO)


def body(
    nx,
    ny,
    mass_hbm,
    alpha_hbm,
    part_hbm,
    kf_hbm,
    kb_hbm,
    out_alpha_ref,
    out_part_ref,
    pu,
    pm,
    pq,
    pe,
    pack,
    gy_in,
    stage,
    s_ref,
    r_ref,
    nu_ref,
    e_ref,
    mass_ref,
    alpha_ref,
    part_ref,
    kf_ref,
    kb_ref,
    load_sem,
    send_sem,
    recv_sem,
):
    gx = lax.axis_index("gx")
    gy = lax.axis_index("gy")
    core = lax.rem(gx, 2)
    near = (gx + 1 - 2 * core, gy)
    far = (lax.rem(gx + nx - 1 + 2 * core, nx), gy)
    before = (gx, lax.rem(gy + ny - 1, ny))
    after = (gx, lax.rem(gy + 1, ny))
    barrier = pltpu.get_barrier_semaphore()
    for target in (near, far, before, after):
        pl.semaphore_signal(barrier, inc=1, device_id=target, device_id_type=MESH)

    loads = [
        pltpu.make_async_copy(src, dst, load_sem.at[i])
        for i, (src, dst) in enumerate(
            (
                (alpha_hbm, alpha_ref),
                (mass_hbm, mass_ref),
                (part_hbm, part_ref),
                (kf_hbm, kf_ref),
                (kb_hbm, kb_ref),
            )
        )
    ]
    for load in loads:
        load.start()

    lane = lanes_of((8, LANES))
    odd = lax.rem(lane, 2) == 1
    even = jnp.logical_not(odd)
    edge = (lane == 0) | (lane == LANES - 1)

    phase_of = [jnp.where(core == c, 1, 0) for c in range(2)]
    u, e, m = [], [], []
    loads[0].wait()
    loads[1].wait()
    for c in range(2):
        alpha = alpha_ref[c]
        top = jnp.max(jnp.max(alpha, axis=0), axis=0, keepdims=True)
        level = up8(jnp.floor(top * LOG2E))
        u.append([jnp.exp((alpha - level[None] * LN2_HI) - level[None] * LN2_LO).reshape(64, LANES)])
        e.append(level)
        mass = mass_ref[c].reshape(64, LANES)
        m.append([mass])
        pm[phase_of[c], 1 - c] = mass
    loads[2].wait()
    for b in range(3):
        z = slice(8 * b, 8 * b + 8)
        for chunk in range(4):
            total = None
            for c in ((0,), (0, 1), (0, 1), (1,))[chunk]:
                y = slice(8 * (chunk - c), 8 * (chunk - c) + 8)
                term = part_ref[c, y, z, :]
                partner = part_ref[c, y, 8:16, :]
                if b == 1:
                    partner = jnp.where(even[None], part_ref[c, y, 0:8, :], part_ref[c, y, 16:24, :])
                total_own = term
                if b == 0:
                    source, mask = part_ref[c, y, 8:16, :], odd
                elif b == 2:
                    source, mask = part_ref[c, y, 8:16, :], even
                else:
                    source = jnp.where(even[None], part_ref[c, y, 16:24, :], part_ref[c, y, 0:8, :])
                    mask = None
                moved = swap(source, even[None])
                if mask is not None:
                    moved = jnp.where(mask[None], moved, 0.0)
                term = total_own + moved
                total = term if total is None else total + term
            nu_ref[b, 8 * chunk : 8 * chunk + 8, :, 0:LANES] = total
    ep = [swap(e[c], even) for c in range(2)]
    weights = [levels(e, ep, even, None)]
    loads[3].wait()
    loads[4].wait()
    for _ in range(ITERS):
        for c in range(2):
            forward_sums(kf_ref, s_ref, c, u[c], [swap(u[c][0], even[0:1])])
        u = backward(kb_ref, r_ref, s_ref, nu_ref, 1, weights, even, m)
    for c in range(2):
        forward_sums(kf_ref, s_ref, c, u[c], [swap(u[c][0], even[0:1])])
    own_w, partner_w, level = weights[0][0], weights[0][1], weights[0][5]
    for chunk in range(4):
        part = (0, 1, 1, 2)[chunk]
        for b in range(3):
            r = ratio_rows(s_ref, nu_ref, 0, chunk, b, own_w, partner_w, even)
            for c in ((0,), (0, 1), (1,))[part]:
                y0 = 8 * (chunk - c)
                root = jnp.exp2(0.5 * (e[c] - level[part][b]))[None]
                value = (s_ref[c, b, y0 : y0 + 8, :, 0:LANES] * root) * (r * root)
                stage[c, 24 * b + y0 : 24 * b + y0 + 8] = value
    for c in range(2):
        stage[c, 72:80] = u[c][0].reshape(8, 8, LANES)
        stage[c, 80:81] = e[c][None]
        stage[c, 81:89] = m[c][0].reshape(8, 8, LANES)
        low, mid, high = stage[c, 0:24], stage[c, 24:48], stage[c, 48:72]
        stage[c, 89:113] = jnp.where((lane == LANES - 1)[None], high, low)
        pu[phase_of[c], 1 - c, 0:64] = u[c][0]
        pu[phase_of[c], 1 - c, 64:72] = e[c]
        moved = swap(jnp.where(odd[None], high, low), odd[None])
        mid = mid + jnp.where(edge[None], 0.0, moved)
        pq[phase_of[c], 1 - c, 0] = jnp.where(odd[None], low, mid)
        pq[phase_of[c], 1 - c, 1] = jnp.where(odd[None], mid, high)

    def pack_step(i, held):
        out = []
        for c in range(2):
            for half in range(2):
                x = stage[c, half * 64 + i]
                x = pltpu.roll(x, 2 * i + 1, axis=1)
                out.append(jnp.where(lax.div(lane, 2) == i, x, held[2 * c + half]))
        return tuple(out)

    for c in range(2):
        stage[c, 113:128] = jnp.zeros((15, 8, LANES), F32)
    zero = jnp.zeros((8, LANES), F32)
    packed = lax.fori_loop(0, 64, pack_step, (zero, zero, zero, zero), unroll=16)
    for c in range(2):
        for half in range(2):
            pack[c, half] = packed[2 * c + half]

    pl.semaphore_wait(barrier, 4)

    def copy(src, dst, sem, target):
        return pltpu.make_async_remote_copy(
            src_ref=src,
            dst_ref=dst,
            send_sem=send_sem.at[sem],
            recv_sem=recv_sem.at[sem],
            device_id=target,
            device_id_type=MESH,
        )

    near_side, far_side = core, 1 - core
    to_before = copy(pack, gy_in.at[1], 0, before)
    to_after = copy(pack, gy_in.at[0], 1, after)
    to_before.start()
    to_after.start()
    sends = {}
    for name, phase, side, target, sem in (
        ("far", 1, far_side, far, 2),
        ("near", 0, near_side, near, 6),
    ):
        for i, buf in enumerate((pu, pq, pm)):
            where = buf.at[phase, side]
            sends[name, i] = copy(where, where, sem + i, target)
            sends[name, i].start()
        where = pe.at[phase, side]
        sends[name, 3] = copy(where, where, sem + 3, target)
    to_before.wait()
    to_after.wait()
    own_entry = (lane >= 2 * (N_HALO - 64))
    for c in range(2):
        for half in range(2):
            merged = jnp.where(even, gy_in[0, c, half], gy_in[1, c, half])
            if half == 1:
                merged = jnp.where(own_entry, pack[c, half], merged)
            pe[phase_of[c], 1 - c, half] = merged
    sends["near", 3].start()
    sends["far", 3].start()

    for phase, name in ((0, "near"), (1, "far")):
        for i in range(4):
            sends[name, i].wait()
        own_side = near_side if phase == 0 else far_side

        def unpack_step(i, _):
            for side in range(2):
                for half in range(2):
                    shift = LANES - (2 * i + 1)
                    stage[side, half * 64 + i] = pltpu.roll(pe[phase, side, half], shift, axis=1)
            return 0

        lax.fori_loop(0, 64, unpack_step, 0, unroll=16)

        for chunk in range(4):
            sides = ((0,), (0, 1), (0, 1), (1,))[chunk]

            def both(read):
                total = None
                for s in sides:
                    term = read(s, 8 * (chunk - s))
                    total = term if total is None else total + term
                return total

            low = both(lambda s, y: pq[phase, s, 0, y : y + 8])
            high = both(lambda s, y: pq[phase, s, 1, y : y + 8])
            ep0, ep1, ep2 = [
                both(lambda s, y, b=b: stage[s, 24 * b + y : 24 * b + y + 8]) for b in range(3)
            ]
            kept = both(lambda s, y: stage[s, 89 + y : 89 + y + 8])
            moved = swap(jnp.where(odd[None], ep2, ep0), odd[None])
            low = low + jnp.where((lane == 0)[None], moved, 0.0)
            high = high + jnp.where((lane == LANES - 1)[None], moved, 0.0)
            other = swap(jnp.where(odd[None], high, low), odd[None])
            other = jnp.where(edge[None], kept + swap(ep1, odd[None]), other)
            rows = slice(8 * chunk, 8 * chunk + 8)
            main, outer = lanes_at(0), lanes_at(1)
            nu_ref[0, rows, :, main] = jnp.where(odd[None], low, other)
            nu_ref[1, rows, :, main] = jnp.where(odd[None], high, low)
            nu_ref[2, rows, :, main] = jnp.where(odd[None], other, high)
            nu_ref[0, rows, :, outer] = jnp.where(odd[None], ep0, swap(high, odd[None]))
            nu_ref[1, rows, :, outer] = swap(other, odd[None])
            nu_ref[2, rows, :, outer] = jnp.where(odd[None], swap(low, odd[None]), ep2)

        u = [[pu[phase, s, 0:64], stage[s, 72:80].reshape(64, LANES)] for s in range(2)]
        e = [[pu[phase, s, 64:72], stage[s, 80]] for s in range(2)]
        m = [[pm[phase, s], stage[s, 81:89].reshape(64, LANES)] for s in range(2)]
        lam = [region_scale(nu_ref, lanes_at(g), odd) for g in range(2)]

        def partners(x, mask, at_edge):
            moved_main, moved_edge = swap(x[0], mask), swap(x[1], mask)
            return [jnp.where(at_edge, moved_edge, moved_main), moved_main]

        for it in range(ITERS + 1):
            for s in range(2):
                forward_sums(kf_ref, s_ref, s, u[s], partners(u[s], odd[0:1], edge[0:1]))
            ep = [partners(e[s], odd, edge) for s in range(2)]
            weights = [
                levels([e[0][g], e[1][g]], [ep[0][g], ep[1][g]], odd, lam[g]) for g in range(2)
            ]
            if it < ITERS:
                u = backward(kb_ref, r_ref, s_ref, nu_ref, 2, weights, odd, m)
                e = [[weights[g][4][s] for g in range(2)] for s in range(2)]

        own_w, partner_w, _, final_w = weights[0][:4]
        own_col = 1 - own_side
        for chunk in range(4):
            for b in range(3):
                r_ref[b, 8 * chunk : 8 * chunk + 8, :, 0:LANES] = ratio_rows(
                    s_ref, nu_ref, 0, chunk, b, own_w, partner_w, odd
                )
        for b in range(3):
            e_ref[0, b] = final_w[0][0][b]
            e_ref[1, b] = final_w[0][1][b]
            e_ref[2, b] = final_w[0][1][b]
            e_ref[3, b] = final_w[1][1][b]
            e_ref[4, b] = final_w[1][1][b]
            e_ref[5, b] = final_w[1][2][b]
        for k in range(3):
            for b in range(3):
                r = r_ref[b, pl.ds(8 * (k + own_side), 8), :, 0:LANES]
                scale = e_ref[3 * own_side + k, b]
                sums = s_ref[own_side, b, 8 * k : 8 * k + 8, :, 0:LANES]
                out_part_ref[own_col, 8 * k : 8 * k + 8, 8 * b : 8 * b + 8, :] = sums * (
                    r * scale[None]
                )
        left = (own_side == 0)
        own_u = jnp.where(left, u[0][0], u[1][0])
        own_e = jnp.where(left, e[0][0], e[1][0])
        out_alpha_ref[own_col] = alpha_of(own_u, own_e).reshape(8, 8, LANES)


def write_out(alpha_in, part_in, alpha_out, part_out, sem):
    copies = [pltpu.make_async_copy(alpha_in, alpha_out, sem.at[0])]
    for c in range(2):
        copies.append(pltpu.make_async_copy(part_in.at[c], part_out.at[c], sem.at[1 + c]))
    for copy in copies:
        copy.start()
    for copy in copies:
        copy.wait()


def per_device(nx, ny, source_mass, alpha_start, part_start):
    forward, back = kernel_tables()
    vmem = pl.BlockSpec(memory_space=pltpu.VMEM)
    results = pl.pallas_call(
        functools.partial(body, nx, ny),
        out_shape=(
            pltpu.VMEM(alpha_start.shape, F32),
            pltpu.VMEM(part_start.shape, F32),
        ),
        in_specs=[pl.BlockSpec(memory_space=pltpu.HBM)] * 5,
        out_specs=(vmem, vmem),
        scratch_shapes=[
            pltpu.VMEM((2, 2, 72, LANES), F32),
            pltpu.VMEM((2, 2, 64, LANES), F32),
            pltpu.VMEM((2, 2, 2, 24, 8, LANES), F32),
            pltpu.VMEM((2, 2, 2, 8, LANES), F32),
            pltpu.VMEM((2, 2, 8, LANES), F32),
            pltpu.VMEM((2, 2, 2, 8, LANES), F32),
            pltpu.VMEM((2, 128, 8, LANES), F32),
            pltpu.VMEM((2, 3, 24, 8, 4 * LANES), F32),
            pltpu.VMEM((3, 32, 8, 4 * LANES), F32),
            pltpu.VMEM((3, 32, 8, 2 * LANES), F32),
            pltpu.VMEM((6, 3, 8, LANES), F32),
            pltpu.VMEM(source_mass.shape, F32),
            pltpu.VMEM(alpha_start.shape, F32),
            pltpu.VMEM(part_start.shape, F32),
            pltpu.VMEM(forward.shape, BF16),
            pltpu.VMEM(back.shape, BF16),
            pltpu.SemaphoreType.DMA((5,)),
            pltpu.SemaphoreType.DMA((10,)),
            pltpu.SemaphoreType.DMA((10,)),
        ],
        compiler_params=pltpu.CompilerParams(
            collective_id=0, has_side_effects=True, vmem_limit_bytes=56 * 2**20
        ),
    )(*[
        pltpu.with_memory_space_constraint(x, pltpu.HBM)
        for x in (source_mass, alpha_start, part_start, jnp.asarray(forward), jnp.asarray(back))
    ])
    anywhere = pl.BlockSpec(memory_space=pl.ANY)
    return pl.pallas_call(
        write_out,
        out_shape=tuple(jax.ShapeDtypeStruct(r.shape, r.dtype) for r in results),
        in_specs=[vmem] * 2,
        out_specs=(anywhere, anywhere),
        scratch_shapes=[pltpu.SemaphoreType.DMA((3,))],
        compiler_params=pltpu.CompilerParams(vmem_limit_bytes=16 * 2**20),
    )(*results)


def solution(mesh):
    placed = P("gx", None, None, "gy")
    return jax.shard_map(
        functools.partial(per_device, mesh.shape["gx"], mesh.shape["gy"]),
        mesh=mesh,
        in_specs=(placed, placed, placed),
        out_specs=(placed, placed),
        check_vma=False,
    )
```

```python
import functools
import math

import jax
import jax.numpy as jnp
import ml_dtypes
import numpy as np
from jax import lax
from jax.experimental import pallas as pl
from jax.experimental.pallas import tpu as pltpu
from jax.sharding import PartitionSpec as P

ITERS = 2
LANES = 128
MESH = pl.DeviceIdType.MESH
LN2_HI = 0.693359375
LN2_LO = math.log(2.0) - 0.693359375
LOG2E = 1.0 / math.log(2.0)
F32 = jnp.float32
BF16 = jnp.bfloat16
EMPTY = -4000.0
TINY = 1.1754944e-38
N_HALO = 89
N_PACK = 113


def kernel_tables():
    a = np.arange(8)[:, None] + 8
    y = np.arange(24)[None, :]
    k1 = np.exp(-((a - y) ** 2) / 32.0)
    full = np.einsum("ay,bz->yzab", k1, k1).reshape(24, 3, 8, 64)
    full = full.transpose(1, 0, 2, 3)
    hi = full.astype(ml_dtypes.bfloat16)
    lo = (full - hi.astype(np.float64)).astype(ml_dtypes.bfloat16)
    forward = np.concatenate([hi, hi, lo], axis=3).reshape(576, 192)
    hi_rows = hi.reshape(3, 192, 64).transpose(0, 2, 1)
    lo_rows = lo.reshape(3, 192, 64).transpose(0, 2, 1)
    backward = np.concatenate([hi_rows, lo_rows], axis=1)
    return forward, backward


def roll_left(x):
    return pltpu.roll(x, LANES - 1, axis=x.ndim - 1)


def roll_right(x):
    return pltpu.roll(x, 1, axis=x.ndim - 1)


def lanes_of(shape):
    return lax.broadcasted_iota(jnp.int32, shape, len(shape) - 1)


def swap(x, first):
    return jnp.where(first, roll_left(x), roll_right(x))


def up8(x):
    return jnp.broadcast_to(x, (8, LANES))


def halves(x):
    hi = x.astype(BF16)
    lo = (x - hi.astype(F32)).astype(BF16)
    return hi, lo


def spread(u):
    hi, lo = halves(u)
    return jnp.concatenate([hi, lo, hi], axis=0)


def levels(e, ep, first, lam):
    sides = ((0,), (0, 1), (1,))
    ex, sh = [], []
    for part in range(3):
        own = [e[s] for s in sides[part]]
        both = own + [ep[s] for s in sides[part]]
        ex.append(functools.reduce(jnp.maximum, own))
        sh.append(functools.reduce(jnp.maximum, both))
    level = [
        [jnp.where(first, ex[p], sh[p]), sh[p], jnp.where(first, sh[p], ex[p])] for p in range(3)
    ]
    own_w, partner_w = [], []
    for p in range(3):
        own_w.append([[jnp.exp2(e[s] - level[p][b]) for b in range(3)] for s in sides[p]])
        rows = []
        for s in sides[p]:
            raw = [jnp.exp2(ep[s] - level[p][b]) for b in range(3)]
            rows.append([jnp.where(first, 0.0, raw[0]), raw[1], jnp.where(first, raw[2], 0.0)])
        partner_w.append(rows)
    if lam is None:
        new_e = [e[0], e[1]]
        lam_b = [[0.0] * 3 for _ in range(3)]
    else:
        lam_ex, lam_sh, lam_b = lam
        new_e = []
        for s, parts in ((0, (0, 1)), (1, (1, 2))):
            top = functools.reduce(
                jnp.maximum, [lam_ex[p] - ex[p] for p in parts] + [lam_sh[p] - sh[p] for p in parts]
            )
            new_e.append(-top)
    out_w, final_w = [], []
    for s, parts in ((0, (0, 1)), (1, (1, 2))):
        out_w.append(
            {p: [jnp.exp2(lam_b[p][b] - level[p][b] + new_e[s]) for b in range(3)] for p in parts}
        )
        final_w.append(
            {p: [jnp.exp2(e[s] - level[p][b] + lam_b[p][b]) for b in range(3)] for p in parts}
        )
    return own_w, partner_w, out_w, final_w, new_e, level


def region_scale(nu_ref, at, first):
    peak = []
    for part, (y0, y1) in enumerate(((0, 8), (8, 24), (24, 32))):
        row = []
        for b in range(3):
            top = jnp.max(nu_ref[b, y0:y1, :, at], axis=0)
            row.append(up8(jnp.max(top, axis=0, keepdims=True)))
        peak.append(row)

    def lg(x):
        exponent = jnp.floor(jnp.log(jnp.maximum(x, TINY)) * LOG2E)
        return jnp.where(x < TINY, EMPTY, exponent)

    lam_ex = [lg(jnp.where(first, peak[p][0], peak[p][2])) for p in range(3)]
    lam_sh = [
        lg(jnp.maximum(peak[p][1], jnp.where(first, peak[p][2], peak[p][0]))) for p in range(3)
    ]
    lam_b = [
        [
            jnp.where(first, lam_ex[p], lam_sh[p]),
            lam_sh[p],
            jnp.where(first, lam_sh[p], lam_ex[p]),
        ]
        for p in range(3)
    ]
    for part, (y0, y1) in enumerate(((0, 8), (8, 24), (24, 32))):
        for b in range(3):
            nu_ref[b, y0:y1, :, at] = nu_ref[b, y0:y1, :, at] * jnp.exp2(
                -jnp.maximum(lam_b[part][b], -125.0)
            )[None]
    return lam_ex, lam_sh, lam_b


def forward_sums(kf_ref, s_ref, side, u, up):
    cols = []
    for g in range(len(u)):
        cols += [u[g], up[g]]
    out = jnp.dot(
        kf_ref[...], spread(jnp.concatenate(cols, axis=1)), preferred_element_type=F32
    )
    s_ref[side, :, :, :, 0 : out.shape[1]] = out.reshape(3, 24, 8, out.shape[1])


def lanes_at(g):
    return slice(g * LANES, (g + 1) * LANES)


def ratio_rows(s_ref, nu_ref, g, chunk, b, own_w, partner_w, first):
    part = (0, 1, 1, 2)[chunk]
    sides = ((0,), (0, 1), (1,))[part]
    own_at, partner_at = lanes_at(2 * g), lanes_at(2 * g + 1)
    total = None
    for i, s in enumerate(sides):
        y0 = 8 * (chunk - s)
        own = s_ref[s, b, y0 : y0 + 8, :, own_at]
        if b == 1:
            partner = jnp.where(
                first[None],
                s_ref[s, 0, y0 : y0 + 8, :, partner_at],
                s_ref[s, 2, y0 : y0 + 8, :, partner_at],
            )
        else:
            partner = s_ref[s, 1, y0 : y0 + 8, :, partner_at]
        term = own * own_w[part][i][b][None] + partner * partner_w[part][i][b][None]
        total = term if total is None else total + term
    return nu_ref[b, 8 * chunk : 8 * chunk + 8, :, lanes_at(g)] / total


def source_sums(kb_ref, r_ref, s_ref, nu_ref, groups, weights, first):
    width = groups * LANES
    for g in range(groups):
        own_w, partner_w, out_w = weights[g][:3]
        for chunk in range(4):
            part = (0, 1, 1, 2)[chunk]
            for b in range(3):
                r = ratio_rows(s_ref, nu_ref, g, chunk, b, own_w, partner_w, first)
                for s in ((0,), (0, 1), (1,))[part]:
                    y0 = 8 * (chunk - s)
                    at = slice(s * width + g * LANES, s * width + (g + 1) * LANES)
                    r_ref[b, y0 : y0 + 8, :, at] = r * out_w[s][part][b][None]
    total = None
    for b in range(3):
        hi, lo = halves(r_ref[b, 0:24, :, 0 : 2 * width].reshape(192, 2 * width))
        top = jnp.dot(kb_ref[b], hi, preferred_element_type=F32)
        low = jnp.dot(kb_ref[b, 0:64, :], lo, preferred_element_type=F32)
        term = top[0:64] + (top[64:128] + low)
        total = term if total is None else total + term
    return [
        [
            total[:, s * width + g * LANES : s * width + (g + 1) * LANES]
            for g in range(groups)
        ]
        for s in range(2)
    ]


def new_potential(total, m):
    return [[m[s][g] / total[s][g] for g in range(len(m[s]))] for s in range(2)]


def alpha_of(u, e):
    shape = u.shape
    e = jnp.broadcast_to(e[None], (shape[0] // 8, 8, LANES)).reshape(shape)
    return e * LN2_HI + (jnp.log(u) + e * LN2_LO)


def body(
    nx,
    ny,
    mass_hbm,
    alpha_hbm,
    part_hbm,
    kf_hbm,
    kb_hbm,
    out_alpha_ref,
    out_part_ref,
    pu,
    pm,
    pq,
    pe,
    pack,
    gy_in,
    stage,
    s_ref,
    r_ref,
    nu_ref,
    e_ref,
    mass_ref,
    alpha_ref,
    part_ref,
    kf_ref,
    kb_ref,
    load_sem,
    send_sem,
    recv_sem,
):
    gx = lax.axis_index("gx")
    gy = lax.axis_index("gy")
    core = lax.rem(gx, 2)
    near = (gx + 1 - 2 * core, gy)
    far = (lax.rem(gx + nx - 1 + 2 * core, nx), gy)
    before = (gx, lax.rem(gy + ny - 1, ny))
    after = (gx, lax.rem(gy + 1, ny))
    barrier = pltpu.get_barrier_semaphore()
    for target in (near, far, before, after):
        pl.semaphore_signal(barrier, inc=1, device_id=target, device_id_type=MESH)

    loads = [
        pltpu.make_async_copy(src, dst, load_sem.at[i])
        for i, (src, dst) in enumerate(
            (
                (alpha_hbm, alpha_ref),
                (mass_hbm, mass_ref),
                (part_hbm, part_ref),
                (kf_hbm, kf_ref),
                (kb_hbm, kb_ref),
            )
        )
    ]
    for load in loads:
        load.start()

    lane = lanes_of((8, LANES))
    odd = lax.rem(lane, 2) == 1
    even = jnp.logical_not(odd)
    edge = (lane == 0) | (lane == LANES - 1)

    phase_of = [jnp.where(core == c, 1, 0) for c in range(2)]
    u, e, m = [], [], []
    loads[0].wait()
    loads[1].wait()
    for c in range(2):
        alpha = alpha_ref[c]
        top = jnp.max(jnp.max(alpha, axis=0), axis=0, keepdims=True)
        level = up8(jnp.floor(top * LOG2E))
        u.append([jnp.exp((alpha - level[None] * LN2_HI) - level[None] * LN2_LO).reshape(64, LANES)])
        e.append(level)
        mass = mass_ref[c].reshape(64, LANES)
        m.append([mass])
        pm[phase_of[c], 1 - c] = mass
    loads[2].wait()
    for b in range(3):
        z = slice(8 * b, 8 * b + 8)
        for chunk in range(4):
            total = None
            for c in ((0,), (0, 1), (0, 1), (1,))[chunk]:
                y = slice(8 * (chunk - c), 8 * (chunk - c) + 8)
                term = part_ref[c, y, z, :]
                partner = part_ref[c, y, 8:16, :]
                if b == 1:
                    partner = jnp.where(even[None], part_ref[c, y, 0:8, :], part_ref[c, y, 16:24, :])
                total_own = term
                if b == 0:
                    source, mask = part_ref[c, y, 8:16, :], odd
                elif b == 2:
                    source, mask = part_ref[c, y, 8:16, :], even
                else:
                    source = jnp.where(even[None], part_ref[c, y, 16:24, :], part_ref[c, y, 0:8, :])
                    mask = None
                moved = swap(source, even[None])
                if mask is not None:
                    moved = jnp.where(mask[None], moved, 0.0)
                term = total_own + moved
                total = term if total is None else total + term
            nu_ref[b, 8 * chunk : 8 * chunk + 8, :, 0:LANES] = total
    ep = [swap(e[c], even) for c in range(2)]
    weights = [levels(e, ep, even, None)]
    loads[3].wait()
    loads[4].wait()
    for _ in range(ITERS):
        for c in range(2):
            forward_sums(kf_ref, s_ref, c, u[c], [swap(u[c][0], even[0:1])])
        u = new_potential(source_sums(kb_ref, r_ref, s_ref, nu_ref, 1, weights, even), m)
    for c in range(2):
        pu[phase_of[c], 1 - c, 0:64] = u[c][0]
        pu[phase_of[c], 1 - c, 64:72] = e[c]

    def copy(src, dst, sem, target):
        return pltpu.make_async_remote_copy(
            src_ref=src,
            dst_ref=dst,
            send_sem=send_sem.at[sem],
            recv_sem=recv_sem.at[sem],
            device_id=target,
            device_id_type=MESH,
        )

    to_before = copy(pack, gy_in.at[1], 0, before)
    to_after = copy(pack, gy_in.at[0], 1, after)
    near_side, far_side = core, 1 - core
    sends = {}
    for name, phase, side, target in (("far", 1, far_side, far), ("near", 0, near_side, near)):
        for i, (key, where) in enumerate(
            (
                ("potential", pu.at[phase, side]),
                ("low", pq.at[phase, side, 0]),
                ("high", pq.at[phase, side, 1]),
                ("edges", pe.at[phase, side]),
                ("mass", pm.at[phase, side]),
            )
        ):
            sends[name, key] = copy(where, where, 2 + 5 * phase + i, target)

    for c in range(2):
        forward_sums(kf_ref, s_ref, c, u[c], [swap(u[c][0], even[0:1])])
    own_w, partner_w, level = weights[0][0], weights[0][1], weights[0][5]
    for chunk in range(4):
        part = (0, 1, 1, 2)[chunk]
        for b in range(3):
            r = ratio_rows(s_ref, nu_ref, 0, chunk, b, own_w, partner_w, even)
            for c in ((0,), (0, 1), (1,))[part]:
                y0 = 8 * (chunk - c)
                root = jnp.exp2(0.5 * (e[c] - level[part][b]))[None]
                value = (s_ref[c, b, y0 : y0 + 8, :, 0:LANES] * root) * (r * root)
                stage[c, 24 * b + y0 : 24 * b + y0 + 8] = value
    for c in range(2):
        low, mid, high = stage[c, 0:24], stage[c, 24:48], stage[c, 48:72]
        moved = swap(jnp.where(odd[None], high, low), odd[None])
        mid = mid + jnp.where(edge[None], 0.0, moved)
        pq[phase_of[c], 1 - c, 0] = jnp.where(odd[None], low, mid)
        pq[phase_of[c], 1 - c, 1] = jnp.where(odd[None], mid, high)
    for c in range(2):
        low, high = stage[c, 0:24], stage[c, 48:72]
        stage[c, 72:80] = u[c][0].reshape(8, 8, LANES)
        stage[c, 80:81] = e[c][None]
        stage[c, 81:89] = m[c][0].reshape(8, 8, LANES)
        stage[c, 89:113] = jnp.where((lane == LANES - 1)[None], high, low)
    for c in range(2):
        for half in range(2):
            held = jnp.zeros((8, LANES), F32)
            for i in range(min(64, N_PACK - 64 * half)):
                x = pltpu.roll(stage[c, half * 64 + i], (2 * i + 1) % LANES, axis=1)
                held = jnp.where((lane == 2 * i) | (lane == 2 * i + 1), x, held)
            pack[c, half] = held

    pl.semaphore_wait(barrier, 4)
    to_before.start()
    to_after.start()
    for key in ("potential", "low", "high"):
        sends["far", key].start()
    for key in ("potential", "low", "high", "mass"):
        sends["near", key].start()
    to_before.wait()
    to_after.wait()
    own_entry = lane >= 2 * (N_HALO - 64)
    for c in range(2):
        for half in range(2):
            merged = jnp.where(even, gy_in[0, c, half], gy_in[1, c, half])
            if half == 1:
                merged = jnp.where(own_entry, pack[c, half], merged)
            pe[phase_of[c], 1 - c, half] = merged
    for key in ("edges", "mass"):
        sends["far", key].start()
    sends["near", "edges"].start()

    for phase, name in ((0, "near"), (1, "far")):
        sends[name, "potential"].wait()
        sends[name, "edges"].wait()
        own_side = near_side if phase == 0 else far_side

        for side in range(2):
            for half in range(2):
                x = pe[phase, side, half]
                for i in range(min(64, N_PACK - 64 * half)):
                    stage[side, half * 64 + i] = pltpu.roll(x, LANES - (2 * i + 1), axis=1)

        u = [[pu[phase, s, 0:64], stage[s, 72:80].reshape(64, LANES)] for s in range(2)]
        e = [[pu[phase, s, 64:72], stage[s, 80]] for s in range(2)]

        def partners(x, mask, at_edge):
            moved_main, moved_edge = swap(x[0], mask), swap(x[1], mask)
            return [jnp.where(at_edge, moved_edge, moved_main), moved_main]

        def beta_sums(u):
            for s in range(2):
                forward_sums(kf_ref, s_ref, s, u[s], partners(u[s], odd[0:1], edge[0:1]))

        beta_sums(u)
        sends[name, "low"].wait()
        sends[name, "high"].wait()
        for chunk in range(4):
            sides = ((0,), (0, 1), (0, 1), (1,))[chunk]

            def both(read):
                total = None
                for s in sides:
                    term = read(s, 8 * (chunk - s))
                    total = term if total is None else total + term
                return total

            low = both(lambda s, y: pq[phase, s, 0, y : y + 8])
            high = both(lambda s, y: pq[phase, s, 1, y : y + 8])
            ep0, ep1, ep2 = [
                both(lambda s, y, b=b: stage[s, 24 * b + y : 24 * b + y + 8]) for b in range(3)
            ]
            kept = both(lambda s, y: stage[s, 89 + y : 89 + y + 8])
            moved = swap(jnp.where(odd[None], ep2, ep0), odd[None])
            low = low + jnp.where((lane == 0)[None], moved, 0.0)
            high = high + jnp.where((lane == LANES - 1)[None], moved, 0.0)
            other = swap(jnp.where(odd[None], high, low), odd[None])
            other = jnp.where(edge[None], kept + swap(ep1, odd[None]), other)
            rows = slice(8 * chunk, 8 * chunk + 8)
            main, outer = lanes_at(0), lanes_at(1)
            nu_ref[0, rows, :, main] = jnp.where(odd[None], low, other)
            nu_ref[1, rows, :, main] = jnp.where(odd[None], high, low)
            nu_ref[2, rows, :, main] = jnp.where(odd[None], other, high)
            nu_ref[0, rows, :, outer] = jnp.where(odd[None], ep0, swap(high, odd[None]))
            nu_ref[1, rows, :, outer] = swap(other, odd[None])
            nu_ref[2, rows, :, outer] = jnp.where(odd[None], swap(low, odd[None]), ep2)

        lam = [region_scale(nu_ref, lanes_at(g), odd) for g in range(2)]

        def masses():
            return [[pm[phase, s], stage[s, 81:89].reshape(64, LANES)] for s in range(2)]

        for it in range(ITERS + 1):
            ep = [partners(e[s], odd, edge) for s in range(2)]
            weights = [
                levels([e[0][g], e[1][g]], [ep[0][g], ep[1][g]], odd, lam[g]) for g in range(2)
            ]
            if it < ITERS:
                total = source_sums(kb_ref, r_ref, s_ref, nu_ref, 2, weights, odd)
                if it == 0:
                    sends[name, "mass"].wait()
                u = new_potential(total, masses())
                e = [[weights[g][4][s] for g in range(2)] for s in range(2)]
                beta_sums(u)

        own_w, partner_w, _, final_w = weights[0][:4]
        own_col = 1 - own_side
        for chunk in range(4):
            for b in range(3):
                r_ref[b, 8 * chunk : 8 * chunk + 8, :, 0:LANES] = ratio_rows(
                    s_ref, nu_ref, 0, chunk, b, own_w, partner_w, odd
                )
        for b in range(3):
            e_ref[0, b] = final_w[0][0][b]
            e_ref[1, b] = final_w[0][1][b]
            e_ref[2, b] = final_w[0][1][b]
            e_ref[3, b] = final_w[1][1][b]
            e_ref[4, b] = final_w[1][1][b]
            e_ref[5, b] = final_w[1][2][b]
        for k in range(3):
            for b in range(3):
                r = r_ref[b, pl.ds(8 * (k + own_side), 8), :, 0:LANES]
                scale = e_ref[3 * own_side + k, b]
                sums = s_ref[own_side, b, 8 * k : 8 * k + 8, :, 0:LANES]
                out_part_ref[own_col, 8 * k : 8 * k + 8, 8 * b : 8 * b + 8, :] = sums * (
                    r * scale[None]
                )
        left = (own_side == 0)
        own_u = jnp.where(left, u[0][0], u[1][0])
        own_e = jnp.where(left, e[0][0], e[1][0])
        out_alpha_ref[own_col] = alpha_of(own_u, own_e).reshape(8, 8, LANES)


def write_out(alpha_in, part_in, alpha_out, part_out, sem):
    copies = [pltpu.make_async_copy(alpha_in, alpha_out, sem.at[0])]
    for c in range(2):
        copies.append(pltpu.make_async_copy(part_in.at[c], part_out.at[c], sem.at[1 + c]))
    for copy in copies:
        copy.start()
    for copy in copies:
        copy.wait()


def per_device(nx, ny, source_mass, alpha_start, part_start):
    forward, back = kernel_tables()
    vmem = pl.BlockSpec(memory_space=pltpu.VMEM)
    results = pl.pallas_call(
        functools.partial(body, nx, ny),
        out_shape=(
            pltpu.VMEM(alpha_start.shape, F32),
            pltpu.VMEM(part_start.shape, F32),
        ),
        in_specs=[pl.BlockSpec(memory_space=pltpu.HBM)] * 5,
        out_specs=(vmem, vmem),
        scratch_shapes=[
            pltpu.VMEM((2, 2, 72, LANES), F32),
            pltpu.VMEM((2, 2, 64, LANES), F32),
            pltpu.VMEM((2, 2, 2, 24, 8, LANES), F32),
            pltpu.VMEM((2, 2, 2, 8, LANES), F32),
            pltpu.VMEM((2, 2, 8, LANES), F32),
            pltpu.VMEM((2, 2, 2, 8, LANES), F32),
            pltpu.VMEM((2, 128, 8, LANES), F32),
            pltpu.VMEM((2, 3, 24, 8, 4 * LANES), F32),
            pltpu.VMEM((3, 32, 8, 4 * LANES), F32),
            pltpu.VMEM((3, 32, 8, 2 * LANES), F32),
            pltpu.VMEM((6, 3, 8, LANES), F32),
            pltpu.VMEM(source_mass.shape, F32),
            pltpu.VMEM(alpha_start.shape, F32),
            pltpu.VMEM(part_start.shape, F32),
            pltpu.VMEM(forward.shape, BF16),
            pltpu.VMEM(back.shape, BF16),
            pltpu.SemaphoreType.DMA((5,)),
            pltpu.SemaphoreType.DMA((12,)),
            pltpu.SemaphoreType.DMA((12,)),
        ],
        compiler_params=pltpu.CompilerParams(
            collective_id=0, has_side_effects=True, vmem_limit_bytes=56 * 2**20
        ),
    )(*[
        pltpu.with_memory_space_constraint(x, pltpu.HBM)
        for x in (source_mass, alpha_start, part_start, jnp.asarray(forward), jnp.asarray(back))
    ])
    anywhere = pl.BlockSpec(memory_space=pl.ANY)
    return pl.pallas_call(
        write_out,
        out_shape=tuple(jax.ShapeDtypeStruct(r.shape, r.dtype) for r in results),
        in_specs=[vmem] * 2,
        out_specs=(anywhere, anywhere),
        scratch_shapes=[pltpu.SemaphoreType.DMA((3,))],
        compiler_params=pltpu.CompilerParams(vmem_limit_bytes=16 * 2**20),
    )(*results)


def solution(mesh):
    placed = P("gx", None, None, "gy")
    return jax.shard_map(
        functools.partial(per_device, mesh.shape["gx"], mesh.shape["gy"]),
        mesh=mesh,
        in_specs=(placed, placed, placed),
        out_specs=(placed, placed),
        check_vma=False,
    )
```

```python
import functools
import math

import jax
import jax.numpy as jnp
import ml_dtypes
import numpy as np
from jax import lax
from jax.experimental import pallas as pl
from jax.experimental.pallas import tpu as pltpu
from jax.sharding import PartitionSpec as P

ITERS = 2
LANES = 128
MESH = pl.DeviceIdType.MESH
LN2_HI = 0.693359375
LN2_LO = math.log(2.0) - 0.693359375
LOG2E = 1.0 / math.log(2.0)
F32 = jnp.float32
BF16 = jnp.bfloat16
EMPTY = -4000.0
TINY = 1.1754944e-38
N_HALO = 89
N_PACK = 113


def kernel_tables():
    a = np.arange(8)[:, None] + 8
    y = np.arange(24)[None, :]
    k1 = np.exp(-((a - y) ** 2) / 32.0)
    full = np.einsum("ay,bz->yzab", k1, k1).reshape(24, 3, 8, 64)
    full = full.transpose(1, 0, 2, 3)
    hi = full.astype(ml_dtypes.bfloat16)
    lo = (full - hi.astype(np.float64)).astype(ml_dtypes.bfloat16)
    forward = np.concatenate([hi, hi, lo], axis=3).reshape(576, 192)
    hi_rows = hi.reshape(3, 192, 64).transpose(0, 2, 1)
    lo_rows = lo.reshape(3, 192, 64).transpose(0, 2, 1)
    backward = np.concatenate([hi_rows, lo_rows], axis=1)
    return forward, backward


def roll_left(x):
    return pltpu.roll(x, LANES - 1, axis=x.ndim - 1)


def roll_right(x):
    return pltpu.roll(x, 1, axis=x.ndim - 1)


def lanes_of(shape):
    return lax.broadcasted_iota(jnp.int32, shape, len(shape) - 1)


def swap(x, first):
    return jnp.where(first, roll_left(x), roll_right(x))


def up8(x):
    return jnp.broadcast_to(x, (8, LANES))


def halves(x):
    hi = x.astype(BF16)
    lo = (x - hi.astype(F32)).astype(BF16)
    return hi, lo


def spread(u):
    hi, lo = halves(u)
    return jnp.concatenate([hi, lo, hi], axis=0)


def levels(e, ep, first, lam):
    sides = ((0,), (0, 1), (1,))
    ex, sh = [], []
    for part in range(3):
        own = [e[s] for s in sides[part]]
        both = own + [ep[s] for s in sides[part]]
        ex.append(functools.reduce(jnp.maximum, own))
        sh.append(functools.reduce(jnp.maximum, both))
    level = [
        [jnp.where(first, ex[p], sh[p]), sh[p], jnp.where(first, sh[p], ex[p])] for p in range(3)
    ]
    own_w, partner_w = [], []
    for p in range(3):
        own_w.append([[jnp.exp2(e[s] - level[p][b]) for b in range(3)] for s in sides[p]])
        rows = []
        for s in sides[p]:
            raw = [jnp.exp2(ep[s] - level[p][b]) for b in range(3)]
            rows.append([jnp.where(first, 0.0, raw[0]), raw[1], jnp.where(first, raw[2], 0.0)])
        partner_w.append(rows)
    if lam is None:
        new_e = [e[0], e[1]]
        lam_b = [[0.0] * 3 for _ in range(3)]
    else:
        lam_ex, lam_sh, lam_b = lam
        new_e = []
        for s, parts in ((0, (0, 1)), (1, (1, 2))):
            top = functools.reduce(
                jnp.maximum, [lam_ex[p] - ex[p] for p in parts] + [lam_sh[p] - sh[p] for p in parts]
            )
            new_e.append(-top)
    out_w, final_w = [], []
    for s, parts in ((0, (0, 1)), (1, (1, 2))):
        out_w.append(
            {p: [jnp.exp2(lam_b[p][b] - level[p][b] + new_e[s]) for b in range(3)] for p in parts}
        )
        final_w.append(
            {p: [jnp.exp2(e[s] - level[p][b] + lam_b[p][b]) for b in range(3)] for p in parts}
        )
    return own_w, partner_w, out_w, final_w, new_e, level


def region_scale(nu_ref, at, first):
    peak = []
    for part, (y0, y1) in enumerate(((0, 8), (8, 24), (24, 32))):
        row = []
        for b in range(3):
            top = jnp.max(nu_ref[b, y0:y1, :, at], axis=0)
            row.append(up8(jnp.max(top, axis=0, keepdims=True)))
        peak.append(row)

    def lg(x):
        exponent = jnp.floor(jnp.log(jnp.maximum(x, TINY)) * LOG2E)
        return jnp.where(x < TINY, EMPTY, exponent)

    lam_ex = [lg(jnp.where(first, peak[p][0], peak[p][2])) for p in range(3)]
    lam_sh = [
        lg(jnp.maximum(peak[p][1], jnp.where(first, peak[p][2], peak[p][0]))) for p in range(3)
    ]
    lam_b = [
        [
            jnp.where(first, lam_ex[p], lam_sh[p]),
            lam_sh[p],
            jnp.where(first, lam_sh[p], lam_ex[p]),
        ]
        for p in range(3)
    ]
    for part, (y0, y1) in enumerate(((0, 8), (8, 24), (24, 32))):
        for b in range(3):
            nu_ref[b, y0:y1, :, at] = nu_ref[b, y0:y1, :, at] * jnp.exp2(
                -jnp.maximum(lam_b[part][b], -125.0)
            )[None]
    return lam_ex, lam_sh, lam_b


def forward_sums(kf_ref, s_ref, side, u, up):
    cols = []
    for g in range(len(u)):
        cols += [u[g], up[g]]
    out = jnp.dot(
        kf_ref[...], spread(jnp.concatenate(cols, axis=1)), preferred_element_type=F32
    )
    s_ref[side, :, :, :, 0 : out.shape[1]] = out.reshape(3, 24, 8, out.shape[1])


def lanes_at(g):
    return slice(g * LANES, (g + 1) * LANES)


def ratio_rows(s_ref, nu_ref, g, chunk, b, own_w, partner_w, first):
    part = (0, 1, 1, 2)[chunk]
    sides = ((0,), (0, 1), (1,))[part]
    own_at, partner_at = lanes_at(2 * g), lanes_at(2 * g + 1)
    total = None
    for i, s in enumerate(sides):
        y0 = 8 * (chunk - s)
        own = s_ref[s, b, y0 : y0 + 8, :, own_at]
        if b == 1:
            partner = jnp.where(
                first[None],
                s_ref[s, 0, y0 : y0 + 8, :, partner_at],
                s_ref[s, 2, y0 : y0 + 8, :, partner_at],
            )
        else:
            partner = s_ref[s, 1, y0 : y0 + 8, :, partner_at]
        term = own * own_w[part][i][b][None] + partner * partner_w[part][i][b][None]
        total = term if total is None else total + term
    return nu_ref[b, 8 * chunk : 8 * chunk + 8, :, lanes_at(g)] / total


def source_sums(kb_ref, r_ref, s_ref, nu_ref, groups, weights, first):
    width = groups * LANES
    for g in range(groups):
        own_w, partner_w, out_w = weights[g][:3]
        for chunk in range(4):
            part = (0, 1, 1, 2)[chunk]
            for b in range(3):
                r = ratio_rows(s_ref, nu_ref, g, chunk, b, own_w, partner_w, first)
                for s in ((0,), (0, 1), (1,))[part]:
                    y0 = 8 * (chunk - s)
                    at = slice(s * width + g * LANES, s * width + (g + 1) * LANES)
                    r_ref[b, y0 : y0 + 8, :, at] = r * out_w[s][part][b][None]
    total = None
    for b in range(3):
        hi, lo = halves(r_ref[b, 0:24, :, 0 : 2 * width].reshape(192, 2 * width))
        top = jnp.dot(kb_ref[b], hi, preferred_element_type=F32)
        low = jnp.dot(kb_ref[b, 0:64, :], lo, preferred_element_type=F32)
        term = top[0:64] + (top[64:128] + low)
        total = term if total is None else total + term
    return [
        [
            total[:, s * width + g * LANES : s * width + (g + 1) * LANES]
            for g in range(groups)
        ]
        for s in range(2)
    ]


def new_potential(total, m):
    return [[m[s][g] / total[s][g] for g in range(len(m[s]))] for s in range(2)]


def alpha_of(u, e):
    shape = u.shape
    e = jnp.broadcast_to(e[None], (shape[0] // 8, 8, LANES)).reshape(shape)
    return e * LN2_HI + (jnp.log(u) + e * LN2_LO)


def body(
    nx,
    ny,
    mass_hbm,
    alpha_hbm,
    part_hbm,
    kf_hbm,
    kb_hbm,
    out_alpha_ref,
    out_part_ref,
    pu,
    pm,
    pq,
    pe,
    pack,
    gy_in,
    above,
    stage,
    s_ref,
    r_ref,
    nu_ref,
    e_ref,
    mass_ref,
    alpha_ref,
    part_ref,
    kf_ref,
    kb_ref,
    load_sem,
    ready_sem,
    send_sem,
    recv_sem,
):
    gx = lax.axis_index("gx")
    gy = lax.axis_index("gy")
    core = lax.rem(gx, 2)
    near = (gx + 1 - 2 * core, gy)
    far = (lax.rem(gx + nx - 1 + 2 * core, nx), gy)
    before = (gx, lax.rem(gy + ny - 1, ny))
    after = (gx, lax.rem(gy + 1, ny))
    barrier = pltpu.get_barrier_semaphore()
    near_before, near_after = (near[0], before[1]), (near[0], after[1])
    far_before, far_after = (far[0], before[1]), (far[0], after[1])
    for target in (near, far, before, near_before, far_before):
        pl.semaphore_signal(barrier, inc=1, device_id=target, device_id_type=MESH)

    loads = [
        pltpu.make_async_copy(src, dst, load_sem.at[i])
        for i, (src, dst) in enumerate(
            (
                (alpha_hbm, alpha_ref),
                (mass_hbm, mass_ref),
                (part_hbm, part_ref),
                (kf_hbm, kf_ref),
                (kb_hbm, kb_ref),
            )
        )
    ]
    for load in loads:
        load.start()

    lane = lanes_of((8, LANES))
    odd = lax.rem(lane, 2) == 1
    even = jnp.logical_not(odd)
    edge = (lane == 0) | (lane == LANES - 1)

    phase_of = [jnp.where(core == c, 1, 0) for c in range(2)]
    u, e, m = [], [], []
    loads[0].wait()
    loads[1].wait()
    for c in range(2):
        alpha = alpha_ref[c]
        top = jnp.max(jnp.max(alpha, axis=0), axis=0, keepdims=True)
        level = up8(jnp.floor(top * LOG2E))
        u.append([jnp.exp((alpha - level[None] * LN2_HI) - level[None] * LN2_LO).reshape(64, LANES)])
        e.append(level)
        mass = mass_ref[c].reshape(64, LANES)
        m.append([mass])
        pm[phase_of[c], 1 - c] = mass
    loads[2].wait()
    for b in range(3):
        z = slice(8 * b, 8 * b + 8)
        for chunk in range(4):
            total = None
            for c in ((0,), (0, 1), (0, 1), (1,))[chunk]:
                y = slice(8 * (chunk - c), 8 * (chunk - c) + 8)
                term = part_ref[c, y, z, :]
                partner = part_ref[c, y, 8:16, :]
                if b == 1:
                    partner = jnp.where(even[None], part_ref[c, y, 0:8, :], part_ref[c, y, 16:24, :])
                total_own = term
                if b == 0:
                    source, mask = part_ref[c, y, 8:16, :], odd
                elif b == 2:
                    source, mask = part_ref[c, y, 8:16, :], even
                else:
                    source = jnp.where(even[None], part_ref[c, y, 16:24, :], part_ref[c, y, 0:8, :])
                    mask = None
                moved = swap(source, even[None])
                if mask is not None:
                    moved = jnp.where(mask[None], moved, 0.0)
                term = total_own + moved
                total = term if total is None else total + term
            nu_ref[b, 8 * chunk : 8 * chunk + 8, :, 0:LANES] = total
    ep = [swap(e[c], even) for c in range(2)]
    weights = [levels(e, ep, even, None)]
    loads[3].wait()
    loads[4].wait()
    for _ in range(ITERS):
        for c in range(2):
            forward_sums(kf_ref, s_ref, c, u[c], [swap(u[c][0], even[0:1])])
        u = new_potential(source_sums(kb_ref, r_ref, s_ref, nu_ref, 1, weights, even), m)
    for c in range(2):
        pu[phase_of[c], 1 - c, 0:64] = u[c][0]
        pu[phase_of[c], 1 - c, 64:72] = e[c]

    def copy(src, dst, sem, target):
        return pltpu.make_async_remote_copy(
            src_ref=src,
            dst_ref=dst,
            send_sem=send_sem.at[sem],
            recv_sem=recv_sem.at[sem],
            device_id=target,
            device_id_type=MESH,
        )

    to_before = copy(pack, gy_in.at[1], 0, before)
    to_after = copy(pack, gy_in.at[0], 1, after)
    near_side, far_side = core, 1 - core
    sends = {}
    for name, phase, side, target in (("far", 1, far_side, far), ("near", 0, near_side, near)):
        for i, (key, where) in enumerate(
            (
                ("potential", pu.at[phase, side]),
                ("low", pq.at[phase, side, 0]),
                ("high", pq.at[phase, side, 1]),
                ("edges", pe.at[phase, side]),
                ("mass", pm.at[phase, side]),
            )
        ):
            sends[name, key] = copy(where, where, 2 + 5 * phase + i, target)

    for c in range(2):
        forward_sums(kf_ref, s_ref, c, u[c], [swap(u[c][0], even[0:1])])
    own_w, partner_w, level = weights[0][0], weights[0][1], weights[0][5]
    for chunk in range(4):
        part = (0, 1, 1, 2)[chunk]
        for b in range(3):
            r = ratio_rows(s_ref, nu_ref, 0, chunk, b, own_w, partner_w, even)
            for c in ((0,), (0, 1), (1,))[part]:
                y0 = 8 * (chunk - c)
                root = jnp.exp2(0.5 * (e[c] - level[part][b]))[None]
                value = (s_ref[c, b, y0 : y0 + 8, :, 0:LANES] * root) * (r * root)
                stage[c, 24 * b + y0 : 24 * b + y0 + 8] = value
    for c in range(2):
        low, mid, high = stage[c, 0:24], stage[c, 24:48], stage[c, 48:72]
        moved = swap(jnp.where(odd[None], high, low), odd[None])
        mid = mid + jnp.where(edge[None], 0.0, moved)
        pq[phase_of[c], 1 - c, 0] = jnp.where(odd[None], low, mid)
        pq[phase_of[c], 1 - c, 1] = jnp.where(odd[None], mid, high)
    for c in range(2):
        low, high = stage[c, 0:24], stage[c, 48:72]
        stage[c, 72:80] = u[c][0].reshape(8, 8, LANES)
        stage[c, 80:81] = e[c][None]
        stage[c, 81:89] = m[c][0].reshape(8, 8, LANES)
        stage[c, 89:113] = jnp.where((lane == LANES - 1)[None], high, low)
    for c in range(2):
        for half in range(2):
            held = jnp.zeros((8, LANES), F32)
            for i in range(min(64, N_PACK - 64 * half)):
                x = pltpu.roll(stage[c, half * 64 + i], (2 * i + 1) % LANES, axis=1)
                held = jnp.where((lane == 2 * i) | (lane == 2 * i + 1), x, held)
            pack[c, half] = held

    pl.semaphore_wait(barrier, 5)
    pl.semaphore_signal(ready_sem, inc=1, device_id=after, device_id_type=MESH)
    to_after.start()
    across = [
        copy(pack.at[1 - core], above.at[0, near_side], 12, near_after),
        copy(pack.at[core], above.at[1, far_side], 13, far_after),
    ]
    across[1].start()
    across[0].start()
    for key in ("potential", "low", "high"):
        sends["far", key].start()
    for key in ("potential", "low", "high", "mass"):
        sends["near", key].start()
    pl.semaphore_wait(ready_sem, 1)
    to_before.start()
    to_before.wait()
    own_entry = lane >= 2 * (N_HALO - 64)
    for c in range(2):
        for half in range(2):
            merged = gy_in[1, c, half]
            if half == 1:
                merged = jnp.where(own_entry, pack[c, half], merged)
            pe[phase_of[c], 1 - c, half] = merged
    for key in ("edges", "mass"):
        sends["far", key].start()
    sends["near", "edges"].start()
    to_after.wait()
    for c in range(2):
        above[phase_of[c], 1 - c] = gy_in[0, c]

    for phase, name in ((0, "near"), (1, "far")):
        sends[name, "potential"].wait()
        sends[name, "edges"].wait()
        across[phase].wait()
        own_side = near_side if phase == 0 else far_side

        for side in range(2):
            for half in range(2):
                from_above = even if half == 0 else even & (lane < 2 * (N_HALO - 64))
                x = jnp.where(from_above, above[phase, side, half], pe[phase, side, half])
                for i in range(min(64, N_PACK - 64 * half)):
                    stage[side, half * 64 + i] = pltpu.roll(x, LANES - (2 * i + 1), axis=1)

        u = [[pu[phase, s, 0:64], stage[s, 72:80].reshape(64, LANES)] for s in range(2)]
        e = [[pu[phase, s, 64:72], stage[s, 80]] for s in range(2)]

        def partners(x, mask, at_edge):
            moved_main, moved_edge = swap(x[0], mask), swap(x[1], mask)
            return [jnp.where(at_edge, moved_edge, moved_main), moved_main]

        def beta_sums(u):
            for s in range(2):
                forward_sums(kf_ref, s_ref, s, u[s], partners(u[s], odd[0:1], edge[0:1]))

        beta_sums(u)
        sends[name, "low"].wait()
        sends[name, "high"].wait()
        for chunk in range(4):
            sides = ((0,), (0, 1), (0, 1), (1,))[chunk]

            def both(read):
                total = None
                for s in sides:
                    term = read(s, 8 * (chunk - s))
                    total = term if total is None else total + term
                return total

            low = both(lambda s, y: pq[phase, s, 0, y : y + 8])
            high = both(lambda s, y: pq[phase, s, 1, y : y + 8])
            ep0, ep1, ep2 = [
                both(lambda s, y, b=b: stage[s, 24 * b + y : 24 * b + y + 8]) for b in range(3)
            ]
            kept = both(lambda s, y: stage[s, 89 + y : 89 + y + 8])
            moved = swap(jnp.where(odd[None], ep2, ep0), odd[None])
            low = low + jnp.where((lane == 0)[None], moved, 0.0)
            high = high + jnp.where((lane == LANES - 1)[None], moved, 0.0)
            other = swap(jnp.where(odd[None], high, low), odd[None])
            other = jnp.where(edge[None], kept + swap(ep1, odd[None]), other)
            rows = slice(8 * chunk, 8 * chunk + 8)
            main, outer = lanes_at(0), lanes_at(1)
            nu_ref[0, rows, :, main] = jnp.where(odd[None], low, other)
            nu_ref[1, rows, :, main] = jnp.where(odd[None], high, low)
            nu_ref[2, rows, :, main] = jnp.where(odd[None], other, high)
            nu_ref[0, rows, :, outer] = jnp.where(odd[None], ep0, swap(high, odd[None]))
            nu_ref[1, rows, :, outer] = swap(other, odd[None])
            nu_ref[2, rows, :, outer] = jnp.where(odd[None], swap(low, odd[None]), ep2)

        lam = [region_scale(nu_ref, lanes_at(g), odd) for g in range(2)]

        def masses():
            return [[pm[phase, s], stage[s, 81:89].reshape(64, LANES)] for s in range(2)]

        for it in range(ITERS + 1):
            ep = [partners(e[s], odd, edge) for s in range(2)]
            weights = [
                levels([e[0][g], e[1][g]], [ep[0][g], ep[1][g]], odd, lam[g]) for g in range(2)
            ]
            if it < ITERS:
                total = source_sums(kb_ref, r_ref, s_ref, nu_ref, 2, weights, odd)
                if it == 0:
                    sends[name, "mass"].wait()
                u = new_potential(total, masses())
                e = [[weights[g][4][s] for g in range(2)] for s in range(2)]
                beta_sums(u)

        own_w, partner_w, _, final_w = weights[0][:4]
        own_col = 1 - own_side
        for chunk in range(4):
            for b in range(3):
                r_ref[b, 8 * chunk : 8 * chunk + 8, :, 0:LANES] = ratio_rows(
                    s_ref, nu_ref, 0, chunk, b, own_w, partner_w, odd
                )
        for b in range(3):
            e_ref[0, b] = final_w[0][0][b]
            e_ref[1, b] = final_w[0][1][b]
            e_ref[2, b] = final_w[0][1][b]
            e_ref[3, b] = final_w[1][1][b]
            e_ref[4, b] = final_w[1][1][b]
            e_ref[5, b] = final_w[1][2][b]
        for k in range(3):
            for b in range(3):
                r = r_ref[b, pl.ds(8 * (k + own_side), 8), :, 0:LANES]
                scale = e_ref[3 * own_side + k, b]
                sums = s_ref[own_side, b, 8 * k : 8 * k + 8, :, 0:LANES]
                out_part_ref[own_col, 8 * k : 8 * k + 8, 8 * b : 8 * b + 8, :] = sums * (
                    r * scale[None]
                )
        left = (own_side == 0)
        own_u = jnp.where(left, u[0][0], u[1][0])
        own_e = jnp.where(left, e[0][0], e[1][0])
        out_alpha_ref[own_col] = alpha_of(own_u, own_e).reshape(8, 8, LANES)


def write_out(alpha_in, part_in, alpha_out, part_out, sem):
    copies = [pltpu.make_async_copy(alpha_in, alpha_out, sem.at[0])]
    for c in range(2):
        copies.append(pltpu.make_async_copy(part_in.at[c], part_out.at[c], sem.at[1 + c]))
    for copy in copies:
        copy.start()
    for copy in copies:
        copy.wait()


def per_device(nx, ny, source_mass, alpha_start, part_start):
    forward, back = kernel_tables()
    vmem = pl.BlockSpec(memory_space=pltpu.VMEM)
    results = pl.pallas_call(
        functools.partial(body, nx, ny),
        out_shape=(
            pltpu.VMEM(alpha_start.shape, F32),
            pltpu.VMEM(part_start.shape, F32),
        ),
        in_specs=[pl.BlockSpec(memory_space=pltpu.HBM)] * 5,
        out_specs=(vmem, vmem),
        scratch_shapes=[
            pltpu.VMEM((2, 2, 72, LANES), F32),
            pltpu.VMEM((2, 2, 64, LANES), F32),
            pltpu.VMEM((2, 2, 2, 24, 8, LANES), F32),
            pltpu.VMEM((2, 2, 2, 8, LANES), F32),
            pltpu.VMEM((2, 2, 8, LANES), F32),
            pltpu.VMEM((2, 2, 2, 8, LANES), F32),
            pltpu.VMEM((2, 2, 2, 8, LANES), F32),
            pltpu.VMEM((2, 128, 8, LANES), F32),
            pltpu.VMEM((2, 3, 24, 8, 4 * LANES), F32),
            pltpu.VMEM((3, 32, 8, 4 * LANES), F32),
            pltpu.VMEM((3, 32, 8, 2 * LANES), F32),
            pltpu.VMEM((6, 3, 8, LANES), F32),
            pltpu.VMEM(source_mass.shape, F32),
            pltpu.VMEM(alpha_start.shape, F32),
            pltpu.VMEM(part_start.shape, F32),
            pltpu.VMEM(forward.shape, BF16),
            pltpu.VMEM(back.shape, BF16),
            pltpu.SemaphoreType.DMA((5,)),
            pltpu.SemaphoreType.REGULAR,
            pltpu.SemaphoreType.DMA((14,)),
            pltpu.SemaphoreType.DMA((14,)),
        ],
        compiler_params=pltpu.CompilerParams(
            collective_id=0, has_side_effects=True, vmem_limit_bytes=56 * 2**20
        ),
    )(*[
        pltpu.with_memory_space_constraint(x, pltpu.HBM)
        for x in (source_mass, alpha_start, part_start, jnp.asarray(forward), jnp.asarray(back))
    ])
    anywhere = pl.BlockSpec(memory_space=pl.ANY)
    return pl.pallas_call(
        write_out,
        out_shape=tuple(jax.ShapeDtypeStruct(r.shape, r.dtype) for r in results),
        in_specs=[vmem] * 2,
        out_specs=(anywhere, anywhere),
        scratch_shapes=[pltpu.SemaphoreType.DMA((3,))],
        compiler_params=pltpu.CompilerParams(vmem_limit_bytes=16 * 2**20),
    )(*results)


def solution(mesh):
    placed = P("gx", None, None, "gy")
    return jax.shard_map(
        functools.partial(per_device, mesh.shape["gx"], mesh.shape["gy"]),
        mesh=mesh,
        in_specs=(placed, placed, placed),
        out_specs=(placed, placed),
        check_vma=False,
    )
```
